32 devices in a mesh: chan: 16 (over z, y, core), patch: 2 (over x).
Axes of the slice: x: 2, y: 2, z: 4, core: 2. Of those that a mesh axis runs over, the one named last changes fastest.
Arguments:
- volume: bfloat16 [2, 2048, 1024], P('patch', 'chan'), may hold values from -6 to 6
- depth_kernel: bfloat16 [27, 2048], P(None, 'chan'), may hold values from -1.25 to 1.25
- mix_weight: bfloat16 [2048, 2048], P('chan'), may hold values from -0.125 to 0.125
- mix_bias: bfloat16 [2048], P('chan'), may hold values from -3 to 3
- out_grad: bfloat16 [2, 2048, 1024], P('patch', 'chan'), may hold values from -1.5 to 1.5
Outputs:
- activated: bfloat16 [2, 2048, 1024], P('patch', 'chan')
- volume_grad: bfloat16 [2, 2048, 1024], P('patch', 'chan')
- kernel_grad: float32 [27, 2048], P(None, 'chan')
- weight_grad: float32 [2048, 2048], P('chan')
- bias_grad: float32 [2048], P('chan')
The draws below stay inside these ranges and needn't reach their ends.
All inputs are finite; a program needn't handle non-finite values.
Results may differ from the reference program's by a relative error of at most 0.011.
Values may be sent and summed in bfloat16 or wider, within the bound.
No kernel may reach another device: no remote copies, remote signals or barrier semaphores. Data moves between devices by JAX's collectives and lax.ppermute only.
A program may use at most 64 MiB of HBM per device.

```python
import jax
import jax.numpy as jnp
from jax import lax

C = 2048
DEPTH = 2
ROWS = 16
SIDE = 32
TAPS = 27
CELLS = 1024
PATCHES = 2


def levels(rng, dims, cuts, low, high):
    def one(axis_at, blocks):
        draws = jax.random.uniform(jax.random.fold_in(jax.random.fold_in(rng, 6), axis_at), (blocks,), jnp.float32, low / len(cuts), high / len(cuts))
        return jnp.repeat(jnp.exp(draws), dims[axis_at] // blocks).reshape((-1,) + (1,) * (len(dims) - axis_at - 1))

    loudness = one(*cuts[0])
    for cut in cuts[1:]:
        loudness = loudness * one(*cut)
    return loudness


def normal_values(rng, shape, deviation, bound, shards=(), kind=jnp.bfloat16):
    level = levels(rng, shape, shards, -0.22, 0.18) if shards else 1.0
    result = jax.random.normal(rng, shape, jnp.float32) * deviation * level
    return jnp.minimum(jnp.maximum(result, -bound), bound).astype(kind)


def setup_inputs(seed: int = 0) -> dict:
    arg_keys = jax.random.split(jax.random.key(seed), 6)
    volume = normal_values(arg_keys[0], (PATCHES, C, CELLS), 1.0, 6.0, ((0, 2), (1, 16)))
    depth_kernel = normal_values(arg_keys[1], (TAPS, C), TAPS ** -0.5, 1.25, ((1, 16),))
    mix_weight = normal_values(arg_keys[2], (C, C), C ** -0.5, 0.125, ((0, 16),))
    mix_bias = normal_values(arg_keys[3], (C,), 0.5, 3.0, ((0, 16),))
    out_grad = normal_values(arg_keys[4], (PATCHES, C, CELLS), 0.25, 1.5, ((0, 2), (1, 16)))
    return {"volume": volume, "depth_kernel": depth_kernel, "mix_weight": mix_weight, "mix_bias": mix_bias, "out_grad": out_grad}


def tap_list():
    return [(step_z, step_y, step_x) for step_z in (-1, 0, 1) for step_y in (-1, 0, 1) for step_x in (-1, 0, 1)]


def shifted(values, step_z, step_y, step_x):
    cell_total = DEPTH * ROWS * SIDE
    offset = step_z * ROWS * SIDE + step_y * SIDE + step_x
    margin = ROWS * SIDE + SIDE + 1
    pad_spec = [(0, 0)] * (values.ndim - 1) + [(margin, margin)]
    padded = jnp.pad(values, pad_spec)
    moved_values = lax.slice_in_dim(padded, margin + offset, margin + offset + cell_total, axis=values.ndim - 1)
    cell_index = jnp.arange(cell_total, dtype=jnp.int32)
    cell_plane = cell_index // (ROWS * SIDE)
    cell_row = (cell_index // SIDE) % ROWS
    cell_column = cell_index % SIDE
    inside = (cell_plane + step_z >= 0) & (cell_plane + step_z < DEPTH)
    inside = inside & (cell_row + step_y >= 0) & (cell_row + step_y < ROWS)
    inside = inside & (cell_column + step_x >= 0) & (cell_column + step_x < SIDE)
    return jnp.where(inside, moved_values, jnp.zeros_like(moved_values))


def depthwise(values, kernel, direction_sign):
    total = jnp.zeros_like(values)
    for tap_index, steps in enumerate(tap_list()):
        moved_values = shifted(values, direction_sign * steps[0], direction_sign * steps[1], direction_sign * steps[2])
        total = total + kernel[tap_index][None, :, None] * moved_values
    return total


def reference(volume, depth_kernel, mix_weight, mix_bias, out_grad):
    vol_float = volume.astype(jnp.float32)
    kernel_float = depth_kernel.astype(jnp.float32)
    mixed_in = depthwise(vol_float, kernel_float, 1).astype(jnp.bfloat16)

    def forward_one(inputs):
        return jnp.dot(mix_weight, inputs, preferred_element_type=jnp.float32)

    pre = lax.map(forward_one, mixed_in) + mix_bias.astype(jnp.float32)[None, :, None]
    gate = jax.nn.sigmoid(pre)
    activated = (pre * gate).astype(jnp.bfloat16)
    pre_grad = (out_grad.astype(jnp.float32) * gate * (1.0 + pre * (1.0 - gate))).astype(jnp.bfloat16)

    def weight_one(operands):
        return jnp.dot(operands[0], operands[1].T, preferred_element_type=jnp.float32)

    weight_grad = jnp.sum(lax.map(weight_one, (pre_grad, mixed_in)), axis=0)
    bias_grad = jnp.sum(pre_grad.astype(jnp.float32), axis=(0, 2))

    def backward_one(grads):
        return jnp.dot(mix_weight.T, grads, preferred_element_type=jnp.float32)

    mixed_grad = lax.map(backward_one, pre_grad).astype(jnp.bfloat16)
    grad_float = mixed_grad.astype(jnp.float32)
    volume_grad = depthwise(grad_float, kernel_float, -1).astype(jnp.bfloat16)
    kernel_rows = [jnp.sum(grad_float * shifted(vol_float, steps[0], steps[1], steps[2]), axis=(0, 2)) for steps in tap_list()]
    kernel_grad = jnp.stack(kernel_rows, axis=0)
    return (activated, volume_grad, kernel_grad, weight_grad, bias_grad)
```

```python
import jax
import jax.numpy as jnp
from jax import lax
from jax.experimental import pallas as pl
from jax.experimental.pallas import tpu as pltpu
from jax.sharding import PartitionSpec as P

DEPTH = 2
ROWS = 16
SIDE = 32
PLANE = ROWS * SIDE
LANES = 128
VREGS = PLANE // LANES
GROUP = 8
STEP_ROWS = 16
TAPS = 27
SMALL_ROWS = 32
MIB = 1024 * 1024


def chip_at(place, chips):
    return jnp.where(place < chips // 2, 2 * place, 2 * (chips - 1 - place) + 1)


def place_of(chip, chips):
    return jnp.where(chip % 2 == 0, chip // 2, chips - 1 - chip // 2)


def lane_index():
    return lax.broadcasted_iota(jnp.int32, (GROUP, LANES), 1)


def column_shift(tiles, step, lane):
    if step == 0:
        return tiles
    inside = lane % SIDE != (SIDE - 1 if step > 0 else 0)
    return [
        jnp.where(inside, pltpu.roll(tile, (-step) % LANES, 1), 0.0) for tile in tiles
    ]


def row_shift(tiles, step, lane):
    if step == 0:
        return tiles
    turned = [pltpu.roll(tile, (-step * SIDE) % LANES, 1) for tile in tiles]
    zero = jnp.zeros_like(tiles[0])
    if step > 0:
        ahead = turned[1:] + [zero]
        return [jnp.where(lane < LANES - SIDE, now, far) for now, far in zip(turned, ahead)]
    behind = [zero] + turned[:-1]
    return [jnp.where(lane >= SIDE, now, far) for now, far in zip(turned, behind)]


def tile_list(values):
    return [values[:, LANES * at : LANES * (at + 1)] for at in range(VREGS)]


def add_tiles(left, right):
    return right if left is None else [a + b for a, b in zip(left, right)]


def scale_tiles(column, tiles):
    return [column * tile for tile in tiles]


def depthwise_kernel(vol_mine, vol_theirs, small_mine, small_theirs, out_ref, taps_ref):
    m = vol_mine.shape[0]
    core = lax.axis_index("chan") % 2
    lane = lane_index()
    same_at = pl.multiple_of(core * PLANE, PLANE)
    other_at = pl.multiple_of((1 - core) * PLANE, PLANE)
    for half, (vol_ref, small_ref) in enumerate(
        ((vol_mine, small_mine), (vol_theirs, small_theirs))
    ):
        taps_ref[half] = small_ref[...].astype(jnp.float32).T

        def group(step, carry):
            at = pl.multiple_of(step * STEP_ROWS, STEP_ROWS)
            same = vol_ref[pl.ds(at, STEP_ROWS), pl.ds(same_at, PLANE)].astype(jnp.float32)
            other = vol_ref[pl.ds(at, STEP_ROWS), pl.ds(other_at, PLANE)].astype(jnp.float32)
            taps = taps_ref[half, pl.ds(at, STEP_ROWS), :]
            parts = []
            for low in range(0, STEP_ROWS, GROUP):
                tap = taps[low : low + GROUP]
                near = tap[:, 9:18]
                far = jnp.where(core == 0, tap[:, 18:27], tap[:, 0:9])
                shifted_same = [
                    column_shift(tile_list(same[low : low + GROUP]), c, lane) for c in (-1, 0, 1)
                ]
                shifted_other = [
                    column_shift(tile_list(other[low : low + GROUP]), c, lane) for c in (-1, 0, 1)
                ]
                total = None
                for b in range(3):
                    row = None
                    for c in range(3):
                        t = 3 * b + c
                        row = add_tiles(row, scale_tiles(near[:, t : t + 1], shifted_same[c]))
                        row = add_tiles(row, scale_tiles(far[:, t : t + 1], shifted_other[c]))
                    total = add_tiles(total, row_shift(row, b - 1, lane))
                parts.append(jnp.concatenate(total, axis=1))
            out_ref[pl.ds(half * m + at, STEP_ROWS), :] = jnp.concatenate(parts, axis=0).astype(
                out_ref.dtype
            )
            return carry

        lax.fori_loop(0, m // STEP_ROWS, group, 0)


def depthwise_forward(vol_mine, vol_theirs, small_mine, small_theirs):
    m = vol_mine.shape[0]
    return pl.pallas_call(
        depthwise_kernel,
        out_shape=jax.ShapeDtypeStruct((2 * m, PLANE), jnp.bfloat16),
        in_specs=[pl.BlockSpec(memory_space=pltpu.VMEM)] * 4,
        out_specs=pl.BlockSpec(memory_space=pltpu.VMEM),
        scratch_shapes=[pltpu.VMEM((2, m, SMALL_ROWS), jnp.float32)],
        compiler_params=pltpu.CompilerParams(vmem_limit_bytes=16 * MIB),
        name="depthwise",
    )(vol_mine, vol_theirs, small_mine, small_theirs)


def mix_kernel(chips, *refs):
    w_mine, w_theirs, w_turned, small_mine, small_theirs, og_mine, og_theirs = refs[:7]
    pieces = refs[7 : 7 + 1 + chips]
    act_mine, act_theirs, grad_ref, right_ref, left_ref, all_ref = refs[8 + chips :]
    m = w_mine.shape[0]
    whole = 2 * m
    index = lax.axis_index("chan")
    core = index % 2
    place = place_of(index // 2, chips)

    def put(owner, half, rows):
        side = core if half == 0 else 1 - core
        all_ref[pl.ds(pl.multiple_of(owner * whole + side * m, m), m), :] = rows

    put(index // 2, 0, pieces[0][:m, :])
    put(index // 2, 1, pieces[0][m:, :])
    for distance in range(1, chips // 2):
        for direction in range(2):
            ref = pieces[2 * distance - 1 + direction]
            back = chips - distance if direction == 0 else distance
            owner = chip_at((place + back) % chips, chips)
            put(owner, 0, ref[:m, :])
            put(owner, 1, ref[m:, :])
    opposite = chip_at((place + chips // 2) % chips, chips)
    put(opposite, 0, pieces[chips - 1][...])
    put(opposite, 1, pieces[chips][...])
    for half, (w_ref, small_ref, og_ref, act_ref) in enumerate(
        (
            (w_mine, small_mine, og_mine, act_mine),
            (w_theirs, small_theirs, og_theirs, act_theirs),
        )
    ):
        bias = small_ref[...].astype(jnp.float32).T[:, TAPS : TAPS + 1]
        pre = jnp.dot(w_ref[...], all_ref[...], preferred_element_type=jnp.float32) + bias
        gate = jax.nn.sigmoid(pre)
        act_ref[...] = (pre * gate).astype(act_ref.dtype)
        grad = og_ref[...].astype(jnp.float32) * gate * (1.0 + pre * (1.0 - gate))
        grad_ref[half * m : (half + 1) * m, :] = grad.astype(grad_ref.dtype)
    block = w_turned[pl.ds(pl.multiple_of(opposite * whole, whole), whole), :]
    first = jnp.dot(block, grad_ref[...], preferred_element_type=jnp.float32)
    right_ref[...] = first[:m].astype(right_ref.dtype)
    left_ref[...] = first[m:].astype(left_ref.dtype)


def mix(chips, w_mine, w_theirs, w_turned, small_mine, small_theirs, og_mine, og_theirs, pieces):
    m = w_mine.shape[0]
    half = jax.ShapeDtypeStruct((m, PLANE), jnp.bfloat16)
    both = jax.ShapeDtypeStruct((2 * m, PLANE), jnp.bfloat16)
    full = jax.ShapeDtypeStruct((2 * m * chips, PLANE), jnp.bfloat16)
    return pl.pallas_call(
        lambda *refs: mix_kernel(chips, *refs),
        out_shape=(half, half, both, half, half, full),
        in_specs=[pl.BlockSpec(memory_space=pltpu.VMEM)] * (7 + len(pieces)),
        out_specs=[pl.BlockSpec(memory_space=pltpu.VMEM)] * 6,
        compiler_params=pltpu.CompilerParams(vmem_limit_bytes=32 * MIB),
        name="mix",
    )(w_mine, w_theirs, w_turned, small_mine, small_theirs, og_mine, og_theirs, *pieces)


def backward_kernel(grad_ref, far_ref, vol_ref, small_ref, out_ref, taps_grad_ref, taps_ref, planes, sums):
    m = vol_ref.shape[0]
    core = lax.axis_index("chan") % 2
    lane = lane_index()
    taps_ref[...] = small_ref[...].astype(jnp.float32).T
    planes[core] = grad_ref[pl.ds(pl.multiple_of(core * m, m), m), :]
    planes[1 - core] = far_ref[...]

    def group(step, carry):
        at = pl.multiple_of(step * STEP_ROWS, STEP_ROWS)
        rows = pl.ds(at, STEP_ROWS)
        vol = [
            vol_ref[rows, z * PLANE : (z + 1) * PLANE].astype(jnp.float32) for z in range(DEPTH)
        ]
        grad = [planes[z, rows, :].astype(jnp.float32) for z in range(DEPTH)]
        taps = taps_ref[rows, :]
        out_parts = [[], []]
        sum_parts = []
        for low in range(0, STEP_ROWS, GROUP):
            tap = taps[low : low + GROUP]
            moved_vol = [
                [column_shift(tile_list(vol[z][low : low + GROUP]), c, lane) for c in (-1, 0, 1)]
                for z in range(DEPTH)
            ]
            moved_grad = [
                [row_shift(tile_list(grad[z][low : low + GROUP]), -b, lane) for b in (-1, 0, 1)]
                for z in range(DEPTH)
            ]
            for z in range(DEPTH):
                total = None
                for c in range(3):
                    column = None
                    for a in (-1, 0, 1):
                        if not 0 <= z - a < DEPTH:
                            continue
                        for b in range(3):
                            t = 9 * (a + 1) + 3 * b + c
                            column = add_tiles(
                                column, scale_tiles(tap[:, t : t + 1], moved_grad[z - a][b])
                            )
                    total = add_tiles(total, column_shift(column, -(c - 1), lane))
                out_parts[z].append(jnp.concatenate(total, axis=1))
            collected = jnp.zeros((GROUP, LANES), jnp.float32)
            for a in (-1, 0, 1):
                for b in range(3):
                    for c in range(3):
                        t = 9 * (a + 1) + 3 * b + c
                        acc = None
                        for z in range(DEPTH):
                            if not 0 <= z + a < DEPTH:
                                continue
                            for left, right in zip(moved_grad[z][b], moved_vol[z + a][c]):
                                acc = left * right if acc is None else acc + left * right
                        collected = jnp.where(
                            lane == t, jnp.sum(acc, axis=1, keepdims=True), collected
                        )
            sum_parts.append(collected)
        for z in range(DEPTH):
            out_ref[rows, z * PLANE : (z + 1) * PLANE] = jnp.concatenate(
                out_parts[z], axis=0
            ).astype(out_ref.dtype)
        sums[rows, :] = jnp.concatenate(sum_parts, axis=0)
        return carry

    lax.fori_loop(0, m // STEP_ROWS, group, 0)
    taps_grad_ref[...] = sums[...].T[:SMALL_ROWS, :]


def depthwise_backward(grad, far, volume, small):
    m = volume.shape[0]
    return pl.pallas_call(
        backward_kernel,
        out_shape=(
            jax.ShapeDtypeStruct((m, DEPTH * PLANE), jnp.bfloat16),
            jax.ShapeDtypeStruct((SMALL_ROWS, m), jnp.float32),
        ),
        in_specs=[pl.BlockSpec(memory_space=pltpu.VMEM)] * 4,
        out_specs=[pl.BlockSpec(memory_space=pltpu.VMEM)] * 2,
        scratch_shapes=[
            pltpu.VMEM((m, SMALL_ROWS), jnp.float32),
            pltpu.VMEM((DEPTH, m, PLANE), jnp.bfloat16),
            pltpu.VMEM((m, LANES), jnp.float32),
        ],
        compiler_params=pltpu.CompilerParams(vmem_limit_bytes=16 * MIB),
        name="depthwise_back",
    )(grad, far, volume, small)


def body(volume, depth_kernel, mix_weight, mix_bias, out_grad):
    n = lax.axis_size("chan")
    patches = lax.axis_size("patch")
    chips = n // 2
    half_ring = chips // 2
    index = lax.axis_index("chan")
    core = index % 2
    chip = index // 2
    place = place_of(chip, chips)
    m = mix_weight.shape[0]
    whole = 2 * m

    ring = [2 * k if k < half_ring else 2 * (chips - 1 - k) + 1 for k in range(chips)]
    to_core = [(i, i ^ 1) for i in range(n)]
    to_right = [
        (2 * ring[k] + c, 2 * ring[(k + 1) % chips] + c) for k in range(chips) for c in range(2)
    ]
    to_left = [(target, source) for source, target in to_right]

    def swap(values):
        return lax.ppermute(values, "chan", to_core)

    def over_patches(values, kind):
        if patches != 2:
            return lax.psum(values, "patch")
        kept = values
        if kind != values.dtype:
            kept = lax.reduce_precision(values, 8, 7)
        came = lax.ppermute(kept.astype(kind), "patch", [(0, 1), (1, 0)])
        return kept + came.astype(values.dtype)

    vol_mine = volume[0]
    small_mine = jnp.concatenate(
        [
            depth_kernel,
            mix_bias[None, :],
            jnp.zeros((SMALL_ROWS - TAPS - 1, m), jnp.bfloat16),
        ],
        axis=0,
    )
    vol_theirs = swap(vol_mine)
    small_theirs = swap(small_mine)
    grad_planes = out_grad[0]
    og_mine = lax.dynamic_slice(grad_planes, (0, core * PLANE), (m, PLANE))
    og_theirs = swap(lax.dynamic_slice(grad_planes, (0, (1 - core) * PLANE), (m, PLANE)))
    w_theirs = swap(mix_weight)
    w_turned = jnp.concatenate([mix_weight, w_theirs], axis=0).T

    mixed_in = depthwise_forward(vol_mine, vol_theirs, small_mine, small_theirs)

    pieces = [mixed_in]
    rightward = leftward = mixed_in
    for step in range(1, half_ring):
        rightward = lax.ppermute(rightward, "chan", to_right)
        leftward = lax.ppermute(leftward, "chan", to_left)
        pieces += [rightward, leftward]
    pieces.append(lax.ppermute(rightward[:m], "chan", to_right))
    pieces.append(lax.ppermute(leftward[m:], "chan", to_left))

    act_mine, act_theirs, pre_grad, rightward, leftward, all_mixed = mix(
        chips, mix_weight, w_theirs, w_turned, small_mine, small_theirs, og_mine, og_theirs, pieces
    )

    rightward = lax.ppermute(rightward, "chan", to_right)
    leftward = lax.ppermute(leftward, "chan", to_left)
    shares = jnp.dot(w_turned, pre_grad, preferred_element_type=jnp.float32)

    def share(distance):
        owner = chip_at((place + distance) % chips, chips)
        return lax.dynamic_slice(shares, (owner * whole, 0), (whole, PLANE))

    for step in range(1, half_ring):
        ahead = share(half_ring - step)
        behind = share(chips - (half_ring - step))
        came_right = rightward.astype(jnp.float32)
        came_left = leftward.astype(jnp.float32)
        if step == 1:
            came_right = jnp.pad(came_right, ((0, m), (0, 0)))
            came_left = jnp.pad(came_left, ((m, 0), (0, 0)))
        rightward = lax.ppermute((ahead + came_right).astype(jnp.bfloat16), "chan", to_right)
        leftward = lax.ppermute((behind + came_left).astype(jnp.bfloat16), "chan", to_left)
    mixed_grad = (
        share(0) + rightward.astype(jnp.float32) + leftward.astype(jnp.float32)
    ).astype(jnp.bfloat16)

    weight_part = lax.dot_general(
        pre_grad, all_mixed, (((1,), (1,)), ((), ())), preferred_element_type=jnp.float32
    )
    weight_sum = weight_part[:m] + swap(weight_part[m:].astype(jnp.bfloat16)).astype(jnp.float32)
    weight_grad = over_patches(weight_sum, jnp.bfloat16)
    bias_part = jnp.sum(pre_grad.astype(jnp.float32), axis=1)
    bias_sum = bias_part[:m] + swap(bias_part[m:])
    act_far = swap(act_theirs)
    activated = jnp.where(
        core == 0,
        jnp.concatenate([act_mine, act_far], axis=1),
        jnp.concatenate([act_far, act_mine], axis=1),
    )

    far = swap(lax.dynamic_slice(mixed_grad, ((1 - core) * m, 0), (m, PLANE)))
    volume_grad, small_grad = depthwise_backward(mixed_grad, far, vol_mine, small_mine)
    small_grad = over_patches(
        jnp.concatenate([small_grad[:TAPS], bias_sum[None, :], small_grad[TAPS + 1 :]], axis=0),
        jnp.float32,
    )
    return (
        activated[None],
        volume_grad[None],
        small_grad[:TAPS],
        weight_grad,
        small_grad[TAPS],
    )


def solution(mesh):
    placed = (
        P("patch", "chan", None),
        P(None, "chan"),
        P("chan", None),
        P("chan"),
        P("patch", "chan", None),
    )
    return jax.shard_map(
        body,
        mesh=mesh,
        in_specs=placed,
        out_specs=(
            P("patch", "chan", None),
            P("patch", "chan", None),
            P(None, "chan"),
            P("chan", None),
            P("chan"),
        ),
        check_vma=False,
    )
```

```python
import jax
import jax.numpy as jnp
from jax import lax
from jax.experimental import pallas as pl
from jax.experimental.pallas import tpu as pltpu
from jax.sharding import PartitionSpec as P

DEPTH = 2
ROWS = 16
SIDE = 32
PLANE = ROWS * SIDE
LANES = 128
VREGS = PLANE // LANES
GROUP = 8
STEP_ROWS = 16
TAPS = 27
TAP_ROWS = 32
BLOCK_ROWS = 32
CHUNKS = 1
CHUNK = PLANE // CHUNKS
MIB = 1024 * 1024


def chip_at(place, chips):
    return jnp.where(place < chips // 2, 2 * place, 2 * (chips - 1 - place) + 1)


def place_of(chip, chips):
    return jnp.where(chip % 2 == 0, chip // 2, chips - 1 - chip // 2)


def lane_index():
    return lax.broadcasted_iota(jnp.int32, (GROUP, LANES), 1)


def column_shift(tiles, step, lane):
    if step == 0:
        return tiles
    inside = lane % SIDE != (SIDE - 1 if step > 0 else 0)
    return [
        jnp.where(inside, pltpu.roll(tile, (-step) % LANES, 1), 0.0) for tile in tiles
    ]


def row_shift(tiles, step, lane):
    if step == 0:
        return tiles
    turned = [pltpu.roll(tile, (-step * SIDE) % LANES, 1) for tile in tiles]
    zero = jnp.zeros_like(tiles[0])
    if step > 0:
        ahead = turned[1:] + [zero]
        return [jnp.where(lane < LANES - SIDE, now, far) for now, far in zip(turned, ahead)]
    behind = [zero] + turned[:-1]
    return [jnp.where(lane >= SIDE, now, far) for now, far in zip(turned, behind)]


def tile_list(values):
    return [values[:, LANES * at : LANES * (at + 1)] for at in range(VREGS)]


def add_tiles(left, right):
    return right if left is None else [a + b for a, b in zip(left, right)]


def scale_tiles(column, tiles):
    wide = jnp.broadcast_to(column, (GROUP, LANES))
    return [wide * tile for tile in tiles]


def tap_columns(kernel_ref):
    taps = kernel_ref[...].astype(jnp.float32)
    pad = jnp.zeros((TAP_ROWS - TAPS, taps.shape[1]), jnp.float32)
    return jnp.concatenate([taps, pad], axis=0).T


def depthwise_rows(vol_ref, taps_ref, at, low_tile, high_tile, core, lane):
    first = max(low_tile - 1, 0)
    wide = min(high_tile + 1, VREGS) - first
    span = wide * LANES
    same_at = pl.multiple_of(core * PLANE + first * LANES, LANES)
    other_at = pl.multiple_of((1 - core) * PLANE + first * LANES, LANES)
    rows = pl.ds(at, STEP_ROWS)
    same = vol_ref[rows, pl.ds(same_at, span)].astype(jnp.float32)
    other = vol_ref[rows, pl.ds(other_at, span)].astype(jnp.float32)
    taps = taps_ref[rows, :]
    parts = []
    for low in range(0, STEP_ROWS, GROUP):
        tap = taps[low : low + GROUP]
        near = tap[:, 9:18]
        far = jnp.where(core == 0, tap[:, 18:27], tap[:, 0:9])
        planes = []
        for values in (same, other):
            tiles = [
                values[low : low + GROUP, LANES * i : LANES * (i + 1)] for i in range(wide)
            ]
            planes.append([column_shift(tiles, c, lane) for c in (-1, 0, 1)])
        total = None
        for b in (-1, 0, 1):
            begin = max(low_tile - (b < 0), 0) - first
            end = min(high_tile + (b > 0), VREGS) - first
            row = None
            for c in range(3):
                t = 3 * (b + 1) + c
                for taps_of, shifts in zip((near, far), planes):
                    row = add_tiles(
                        row, scale_tiles(taps_of[:, t : t + 1], shifts[c][begin:end])
                    )
            moved = row_shift(row, b, lane)
            moved = moved[low_tile - first - begin :][: high_tile - low_tile]
            total = add_tiles(total, moved)
        parts.append(jnp.concatenate(total, axis=1))
    return jnp.concatenate(parts, axis=0).astype(jnp.bfloat16)


def each_rows(m, step, unroll):
    size = min(unroll * STEP_ROWS, m)

    def run(index, carry):
        for at in range(0, size, STEP_ROWS):
            step(pl.multiple_of(index * size + at, STEP_ROWS))
        return carry

    lax.fori_loop(0, m // size, run, 0)


def depthwise_own_kernel(vol_hbm, kernel_hbm, *refs):
    outs = refs[:CHUNKS]
    vol_ref, kernel_ref, taps_ref, sems = refs[CHUNKS:]
    m = vol_ref.shape[0]
    rows = min(BLOCK_ROWS, m)
    core = lax.axis_index("chan") % 2
    lane = lane_index()
    taps_copy = pltpu.make_async_copy(kernel_hbm, kernel_ref, sems.at[0])
    taps_copy.start()
    copies = [
        pltpu.make_async_copy(
            vol_hbm.at[pl.ds(at, rows)], vol_ref.at[pl.ds(at, rows)], sems.at[1 + at // rows]
        )
        for at in range(0, m, rows)
    ]
    for copy in copies:
        copy.start()
    taps_copy.wait()
    taps_ref[...] = tap_columns(kernel_ref)
    for block, copy in enumerate(copies):
        copy.wait()
        for at in range(block * rows, (block + 1) * rows, STEP_ROWS):
            result = depthwise_rows(vol_ref, taps_ref, at, 0, VREGS, core, lane)
            for chunk in range(CHUNKS):
                outs[chunk][at : at + STEP_ROWS, :] = result[:, chunk * CHUNK : (chunk + 1) * CHUNK]


def depthwise_theirs_kernel(chunk, vol_ref, kernel_ref, own_ref, out_ref, taps_ref):
    m = vol_ref.shape[0]
    core = lax.axis_index("chan") % 2
    lane = lane_index()
    taps_ref[...] = tap_columns(kernel_ref)
    out_ref[:m, :] = own_ref[...]
    low, high = chunk * CHUNK // LANES, (chunk + 1) * CHUNK // LANES

    def step(at):
        out_ref[pl.ds(m + at, STEP_ROWS), :] = depthwise_rows(
            vol_ref, taps_ref, at, low, high, core, lane
        )

    each_rows(m, step, 2)


VMEM_SPEC = pl.BlockSpec(memory_space=pltpu.VMEM)
HBM_SPEC = pl.BlockSpec(memory_space=pltpu.HBM)


ANY_SPEC = pl.BlockSpec(memory_space=pl.ANY)


def vmem_call(kernel, operands, outs, name, scratch=(), alias=None, spec=VMEM_SPEC, free=0):
    if spec is HBM_SPEC:
        operands = [pltpu.with_memory_space_constraint(x, pltpu.HBM) for x in operands]
    return pl.pallas_call(
        kernel,
        out_shape=outs,
        in_specs=[ANY_SPEC] * free + [spec] * (len(operands) - free),
        out_specs=[VMEM_SPEC] * len(outs),
        scratch_shapes=list(scratch),
        input_output_aliases=alias or {},
        compiler_params=pltpu.CompilerParams(vmem_limit_bytes=12 * MIB),
        name=name,
    )(*operands)


def position(chips):
    index = lax.axis_index("chan")
    return index % 2, index // 2, place_of(index // 2, chips)


def turn_kernel(mine, theirs, straight, turned):
    m = mine.shape[0]
    straight[:m, :] = mine[...]
    straight[m:, :] = theirs[...]
    turned[:, :m] = mine[...].T
    turned[:, m:] = theirs[...].T


def product(weights, block):
    return jnp.dot(weights, block, preferred_element_type=jnp.float32)


def stash(rows, all_ref, owner, half, chunk, core, m):
    side = core if half == 0 else 1 - core
    at = pl.multiple_of(owner * (2 * m) + side * m, m)
    all_ref[pl.ds(at, m), chunk * CHUNK : (chunk + 1) * CHUNK] = rows


def assemble_kernel(chips, chunk, *refs):
    pieces = refs[: chips - 1]
    all_ref, sems = refs[-2:]
    core, chip, place = position(chips)
    m = pieces[0].shape[0] // 2
    copies = []
    for number, piece in enumerate(pieces):
        distance = (number + 1) // 2
        back = chips - distance if number % 2 == 1 else distance
        owner = chip_at((place + back) % chips, chips)
        for half in range(2):
            side = core if half == 0 else 1 - core
            at = pl.multiple_of(owner * (2 * m) + side * m, m)
            copy = pltpu.make_async_copy(
                piece.at[pl.ds(half * m, m)],
                all_ref.at[pl.ds(at, m), pl.ds(chunk * CHUNK, CHUNK)],
                sems.at[len(copies)],
            )
            copy.start()
            copies.append(copy)
    for copy in copies:
        copy.wait()


def bias_column(ref):
    return jnp.broadcast_to(ref[...].astype(jnp.float32), (GROUP, ref.shape[1])).T[:, 0:1]


def weight_rows(turned, owner, whole):
    return turned[pl.ds(pl.multiple_of(owner * whole, whole), whole), :]


def mix_kernel(
    chips, chunk, straight, turned, right, left, bias_mine, bias_theirs, og_mine, og_theirs, *refs
):
    act_mine, act_theirs, grad_ref, all_ref, right_ref, left_ref = refs[-6:]
    core, _, place = position(chips)
    m = right.shape[0]
    lanes = slice(chunk * CHUNK, (chunk + 1) * CHUNK)
    opposite = chip_at((place + chips // 2) % chips, chips)
    stash(right[...], all_ref, opposite, 0, chunk, core, m)
    stash(left[...], all_ref, opposite, 1, chunk, core, m)
    sums = product(straight[...], all_ref[:, lanes])
    for half, (bias_ref, og_ref, act_ref) in enumerate(
        ((bias_mine, og_mine, act_mine), (bias_theirs, og_theirs, act_theirs))
    ):
        rows = slice(half * m, (half + 1) * m)
        pre = sums[rows] + bias_column(bias_ref)
        gate = jax.nn.sigmoid(pre)
        act_ref[:, lanes] = (pre * gate).astype(act_ref.dtype)
        grad = og_ref[:, lanes].astype(jnp.float32) * gate * (1.0 + pre * (1.0 - gate))
        grad_ref[rows, lanes] = grad.astype(grad_ref.dtype)
    share = product(weight_rows(turned, opposite, 2 * m), grad_ref[:, lanes])
    right_ref[...] = share[:m].astype(right_ref.dtype)
    left_ref[...] = share[m:].astype(left_ref.dtype)


def pass_kernel(chips, chunk, distance, half, turned, grad, came, out_ref):
    _, _, place = position(chips)
    whole = grad.shape[0]
    m = whole // 2
    values = grad[:, chunk * CHUNK : (chunk + 1) * CHUNK]
    ahead = distance if half == 0 else chips - distance
    owner = chip_at((place + ahead) % chips, chips)
    share = product(weight_rows(turned, owner, whole), values)
    if came.shape[0] == whole:
        out_ref[...] = (share + came[...].astype(jnp.float32)).astype(out_ref.dtype)
    else:
        for side in range(2):
            rows = slice(side * m, (side + 1) * m)
            part = share[rows]
            if side == half:
                part = part + came[...].astype(jnp.float32)
            out_ref[rows, :] = part.astype(out_ref.dtype)


def last_kernel(chips, chunk, turned, grad, right, left, mine_ref, theirs_ref):
    core, chip, _ = position(chips)
    m = mine_ref.shape[0]
    total = (
        product(
            weight_rows(turned, chip, 2 * m), grad[:, chunk * CHUNK : (chunk + 1) * CHUNK]
        )
        + right[...].astype(jnp.float32)
        + left[...].astype(jnp.float32)
    )
    mine_ref[...] = jnp.where(core == 0, total[:m], total[m:]).astype(mine_ref.dtype)
    theirs_ref[...] = jnp.where(core == 0, total[m:], total[:m]).astype(theirs_ref.dtype)


LANE_PAIRS = (((1,), (1,)), ((), ()))


def weight_theirs_kernel(grad, all_ref, out_ref, bias_ref):
    m = out_ref.shape[0]
    out_ref[...] = lax.dot_general(
        grad[m:, :], all_ref[...], LANE_PAIRS, preferred_element_type=jnp.float32
    ).astype(out_ref.dtype)
    ones = jnp.ones((GROUP, PLANE), grad.dtype)
    bias_ref[...] = lax.dot_general(
        ones, grad[...], LANE_PAIRS, preferred_element_type=jnp.float32
    )


def weight_mine_kernel(grad, all_ref, came, out_ref):
    m = out_ref.shape[0]
    total = lax.dot_general(
        grad[:m, :], all_ref[...], LANE_PAIRS, preferred_element_type=jnp.float32
    )
    out_ref[...] = (total + came[...].astype(jnp.float32)).astype(out_ref.dtype)


def plane_order(core, chunks, planes):
    for which, side in ((0, core), (1, 1 - core)):
        for chunk in range(CHUNKS):
            planes[side, :, chunk * CHUNK : (chunk + 1) * CHUNK] = chunks[which * CHUNKS + chunk][
                ...
            ]


def tap_grad_kernel(*refs):
    vol_ref, bias_ref, bias_far, out_ref, planes, sums = refs[2 * CHUNKS :]
    m = vol_ref.shape[0]
    lane = lane_index()
    plane_order(lax.axis_index("chan") % 2, refs[: 2 * CHUNKS], planes)

    def group(at):
        rows = pl.ds(at, STEP_ROWS)
        vol = [
            vol_ref[rows, z * PLANE : (z + 1) * PLANE].astype(jnp.float32) for z in range(DEPTH)
        ]
        grad = [planes[z, rows, :].astype(jnp.float32) for z in range(DEPTH)]
        sum_parts = []
        for low in range(0, STEP_ROWS, GROUP):
            moved_vol = [
                [column_shift(tile_list(vol[z][low : low + GROUP]), c, lane) for c in (-1, 0, 1)]
                for z in range(DEPTH)
            ]
            moved_grad = [
                [row_shift(tile_list(grad[z][low : low + GROUP]), -b, lane) for b in (-1, 0, 1)]
                for z in range(DEPTH)
            ]
            collected = jnp.zeros((GROUP, LANES), jnp.float32)
            for a in (-1, 0, 1):
                for b in range(3):
                    for c in range(3):
                        t = 9 * (a + 1) + 3 * b + c
                        acc = None
                        for z in range(DEPTH):
                            if not 0 <= z + a < DEPTH:
                                continue
                            for left, right in zip(moved_grad[z][b], moved_vol[z + a][c]):
                                acc = left * right if acc is None else acc + left * right
                        collected = jnp.where(
                            lane == t, jnp.sum(acc, axis=1, keepdims=True), collected
                        )
            sum_parts.append(collected)
        sums[rows, :] = jnp.concatenate(sum_parts, axis=0)

    each_rows(m, group, 1)
    out_ref[:TAPS, :] = sums[...].T[:TAPS, :]
    out_ref[TAPS : TAPS + 1, :] = bias_ref[0:1, :m] + bias_far[0:1, :]


def volume_grad_kernel(*refs):
    kernel_ref, out_ref, planes, taps_ref = refs[2 * CHUNKS :]
    m = out_ref.shape[0]
    lane = lane_index()
    plane_order(lax.axis_index("chan") % 2, refs[: 2 * CHUNKS], planes)
    taps_ref[...] = tap_columns(kernel_ref)

    def group(at):
        rows = pl.ds(at, STEP_ROWS)
        grad = [planes[z, rows, :].astype(jnp.float32) for z in range(DEPTH)]
        taps = taps_ref[rows, :]
        out_parts = [[], []]
        for low in range(0, STEP_ROWS, GROUP):
            tap = taps[low : low + GROUP]
            moved_grad = [
                [row_shift(tile_list(grad[z][low : low + GROUP]), -b, lane) for b in (-1, 0, 1)]
                for z in range(DEPTH)
            ]
            for z in range(DEPTH):
                total = None
                for c in range(3):
                    column = None
                    for a in (-1, 0, 1):
                        if not 0 <= z - a < DEPTH:
                            continue
                        for b in range(3):
                            t = 9 * (a + 1) + 3 * b + c
                            column = add_tiles(
                                column, scale_tiles(tap[:, t : t + 1], moved_grad[z - a][b])
                            )
                    total = add_tiles(total, column_shift(column, -(c - 1), lane))
                out_parts[z].append(jnp.concatenate(total, axis=1))
        for z in range(DEPTH):
            out_ref[rows, z * PLANE : (z + 1) * PLANE] = jnp.concatenate(
                out_parts[z], axis=0
            ).astype(out_ref.dtype)

    each_rows(m, group, 1)


def body(volume, depth_kernel, mix_weight, mix_bias, out_grad):
    n = lax.axis_size("chan")
    patches = lax.axis_size("patch")
    chips = n // 2
    half_ring = chips // 2
    core = lax.axis_index("chan") % 2
    m, channels = mix_weight.shape
    whole = 2 * m

    ring = [2 * k if k < half_ring else 2 * (chips - 1 - k) + 1 for k in range(chips)]
    to_core = [(i, i ^ 1) for i in range(n)]
    to_right = [
        (2 * ring[k] + c, 2 * ring[(k + 1) % chips] + c) for k in range(chips) for c in range(2)
    ]
    to_left = [(target, source) for source, target in to_right]

    def shape(rows, columns, kind=jnp.bfloat16):
        return jax.ShapeDtypeStruct((rows, columns), kind)

    def swap(values):
        return lax.ppermute(values, "chan", to_core)

    def send(right, left):
        return lax.ppermute(right, "chan", to_right), lax.ppermute(left, "chan", to_left)

    def over_patches(values):
        if patches != 2:
            return lax.psum(values.astype(jnp.float32), "patch")
        came = lax.ppermute(values, "patch", [(0, 1), (1, 0)])
        return values.astype(jnp.float32) + came.astype(jnp.float32)

    block_rows = min(BLOCK_ROWS, m)
    vol_mine = volume[0]
    vol_theirs = swap(vol_mine)
    kernel_theirs = swap(depth_kernel)
    taps_scratch = pltpu.VMEM((m, TAP_ROWS), jnp.float32)
    mixed_own = vmem_call(
        depthwise_own_kernel,
        (vol_mine, depth_kernel),
        (shape(m, CHUNK),) * CHUNKS,
        "depthwise_own",
        scratch=(
            pltpu.VMEM(vol_mine.shape, jnp.bfloat16),
            pltpu.VMEM(depth_kernel.shape, jnp.bfloat16),
            taps_scratch,
            pltpu.SemaphoreType.DMA((1 + m // block_rows,)),
        ),
        spec=HBM_SPEC,
    )
    mixed_in = []
    for chunk in range(CHUNKS):
        (both,) = vmem_call(
            lambda *refs, chunk=chunk: depthwise_theirs_kernel(chunk, *refs),
            (vol_theirs, kernel_theirs, mixed_own[chunk]),
            (shape(whole, CHUNK),),
            "depthwise_theirs",
            scratch=(taps_scratch,),
        )
        mixed_in.append(both)

    bias_mine = mix_bias[None, :]
    bias_theirs = swap(bias_mine)
    grad_planes = out_grad[0]
    og_mine = lax.dynamic_slice(grad_planes, (0, core * PLANE), (m, PLANE))
    og_theirs = swap(lax.dynamic_slice(grad_planes, (0, (1 - core) * PLANE), (m, PLANE)))
    straight, turned = vmem_call(
        turn_kernel,
        (mix_weight, swap(mix_weight)),
        (shape(whole, channels), shape(channels, whole)),
        "turn",
    )

    all_shape = shape(channels, PLANE)
    flying = [(values, values) for values in mixed_in]
    pieces = [[values] for values in mixed_in]
    for step in range(1, half_ring):
        for chunk in range(CHUNKS):
            flying[chunk] = send(*flying[chunk])
            pieces[chunk] += flying[chunk]
    for chunk in range(CHUNKS):
        right, left = flying[chunk]
        flying[chunk] = send(right[:m], left[m:])
    filled = ()
    for chunk in range(CHUNKS):
        filled = vmem_call(
            lambda *refs, chunk=chunk: assemble_kernel(chips, chunk, *refs),
            (*pieces[chunk], *filled),
            (all_shape,),
            "assemble",
            scratch=(pltpu.SemaphoreType.DMA((2 * (chips - 1),)),),
            alias={chips - 1: 0} if filled else None,
            free=chips - 1,
        )
    made = ()
    for chunk in range(CHUNKS):
        before = (*made, *filled)
        act_mine, act_theirs, pre_grad, all_mixed, right, left = vmem_call(
            lambda *refs, chunk=chunk: mix_kernel(chips, chunk, *refs),
            (
                straight,
                turned,
                *flying[chunk],
                bias_mine,
                bias_theirs,
                og_mine,
                og_theirs,
                *before,
            ),
            (
                shape(m, PLANE),
                shape(m, PLANE),
                shape(whole, PLANE),
                all_shape,
                shape(m, CHUNK),
                shape(m, CHUNK),
            ),
            "mix",
            alias={8: 3} if not made else {8 + i: i for i in range(4)},
        )
        made, filled = (act_mine, act_theirs, pre_grad), (all_mixed,)
        flying[chunk] = (right, left, pre_grad)

    weight_shape = shape(m, channels)
    weight_theirs, bias_part = vmem_call(
        weight_theirs_kernel,
        (pre_grad, all_mixed),
        (weight_shape, shape(GROUP, whole, jnp.float32)),
        "weight_theirs",
    )
    weight_far = swap(weight_theirs)
    bias_far = swap(bias_part[:, m:])
    act_far = swap(act_theirs)
    (weight_sum,) = vmem_call(
        weight_mine_kernel, (pre_grad, all_mixed, weight_far), (weight_shape,), "weight_mine"
    )
    weight_grad = over_patches(weight_sum)
    activated = jnp.where(
        core == 0,
        jnp.concatenate([act_mine, act_far], axis=1),
        jnp.concatenate([act_far, act_mine], axis=1),
    )
    for step in range(1, half_ring):
        for chunk in range(CHUNKS):
            *values, grad = flying[chunk]
            values = send(*values)
            flying[chunk] = [
                vmem_call(
                    lambda *refs, chunk=chunk, step=step, half=half: pass_kernel(
                        chips, chunk, half_ring - step, half, *refs
                    ),
                    (turned, grad, values[half]),
                    (shape(whole, CHUNK),),
                    "pass",
                )[0]
                for half in range(2)
            ] + [grad]
    near, far = [], []
    for chunk in range(CHUNKS):
        right, left, grad = flying[chunk]
        right, left = send(right, left)
        mine, theirs = vmem_call(
            lambda *refs, chunk=chunk: last_kernel(chips, chunk, *refs),
            (turned, grad, right, left),
            (shape(m, CHUNK),) * 2,
            "last",
        )
        near.append(mine)
        far.append(swap(theirs))

    planes = pltpu.VMEM((DEPTH, m, PLANE), jnp.bfloat16)
    (kernel_grad,) = vmem_call(
        tap_grad_kernel,
        (*near, *far, vol_mine, bias_part, bias_far),
        (shape(TAPS + 1, m, jnp.float32),),
        "tap_grad",
        scratch=(planes, pltpu.VMEM((m, LANES), jnp.float32)),
    )
    kernel_grad = over_patches(kernel_grad)
    (volume_grad,) = vmem_call(
        volume_grad_kernel,
        (*near, *far, depth_kernel),
        (shape(m, DEPTH * PLANE),),
        "volume_grad",
        scratch=(planes, taps_scratch),
    )
    return (
        activated[None],
        volume_grad[None],
        kernel_grad[:TAPS],
        weight_grad,
        kernel_grad[TAPS],
    )


def solution(mesh):
    placed = (
        P("patch", "chan", None),
        P(None, "chan"),
        P("chan", None),
        P("chan"),
        P("patch", "chan", None),
    )
    return jax.shard_map(
        body,
        mesh=mesh,
        in_specs=placed,
        out_specs=(
            P("patch", "chan", None),
            P("patch", "chan", None),
            P(None, "chan"),
            P("chan", None),
            P("chan"),
        ),
        check_vma=False,
    )
```

```python
import jax
import jax.numpy as jnp
from jax import lax
from jax.experimental import pallas as pl
from jax.experimental.pallas import tpu as pltpu
from jax.sharding import PartitionSpec as P

DEPTH = 2
ROWS = 16
SIDE = 32
PLANE = ROWS * SIDE
LANES = 128
VREGS = PLANE // LANES
GROUP = 8
STEP_ROWS = 16
TAPS = 27
TAP_ROWS = 32
BLOCK_ROWS = 32
MIB = 1024 * 1024


def chip_at(place, chips):
    return jnp.where(place < chips // 2, 2 * place, 2 * (chips - 1 - place) + 1)


def place_of(chip, chips):
    return jnp.where(chip % 2 == 0, chip // 2, chips - 1 - chip // 2)


def lane_index():
    return lax.broadcasted_iota(jnp.int32, (GROUP, LANES), 1)


def column_shift(tiles, step, lane):
    if step == 0:
        return tiles
    inside = lane % SIDE != (SIDE - 1 if step > 0 else 0)
    return [
        jnp.where(inside, pltpu.roll(tile, (-step) % LANES, 1), 0.0) for tile in tiles
    ]


def row_shift(tiles, step, lane):
    if step == 0:
        return tiles
    turned = [pltpu.roll(tile, (-step * SIDE) % LANES, 1) for tile in tiles]
    zero = jnp.zeros_like(tiles[0])
    if step > 0:
        ahead = turned[1:] + [zero]
        return [jnp.where(lane < LANES - SIDE, now, far) for now, far in zip(turned, ahead)]
    behind = [zero] + turned[:-1]
    return [jnp.where(lane >= SIDE, now, far) for now, far in zip(turned, behind)]


def tile_list(values):
    return [values[:, LANES * at : LANES * (at + 1)] for at in range(VREGS)]


def add_tiles(left, right):
    return right if left is None else [a + b for a, b in zip(left, right)]


def scale_tiles(column, tiles):
    wide = jnp.broadcast_to(column, (GROUP, LANES))
    return [wide * tile for tile in tiles]


def tap_columns(kernel_ref):
    taps = kernel_ref[...].astype(jnp.float32)
    core = lax.axis_index("chan") % 2
    down, same, up = taps[0:9], taps[9:18], taps[18:27]
    pad = jnp.zeros((TAP_ROWS - TAPS, taps.shape[1]), jnp.float32)
    order = [same, jnp.where(core == 0, up, down), jnp.where(core == 0, down, up), pad]
    return jnp.concatenate(order, axis=0).T


def spread_taps(kernel_ref, wide_ref):
    columns = tap_columns(kernel_ref)
    for t in range(wide_ref.shape[0]):
        wide_ref[t] = jnp.broadcast_to(columns[:, t : t + 1], (columns.shape[0], LANES))


def spread_kernel(kernel_ref, wide_ref):
    spread_taps(kernel_ref, wide_ref)


def depthwise_rows(vol_ref, wide_ref, at, core, lane):
    rows = pl.ds(at, STEP_ROWS)
    sources = [
        vol_ref[rows, pl.ds(pl.multiple_of(plane * PLANE, PLANE), PLANE)].astype(jnp.float32)
        for plane in (core, 1 - core)
    ]
    parts = []
    for low in range(0, STEP_ROWS, GROUP):
        group = pl.ds(at + low, GROUP)
        tiles = [tile_list(values[low : low + GROUP]) for values in sources]
        moved = [[column_shift(plane, c, lane) for c in (-1, 0, 1)] for plane in tiles]
        lines = [None] * 3
        for b in range(3):
            for side in range(2):
                for c in range(3):
                    wide = wide_ref[9 * side + 3 * b + c, group, :]
                    lines[b] = add_tiles(lines[b], [wide * tile for tile in moved[side][c]])
        shifted = [row_shift(lines[b], b - 1, lane) for b in (0, 2)]
        total = add_tiles(add_tiles(lines[1], shifted[0]), shifted[1])
        parts.append(jnp.concatenate(total, axis=1))
    return jnp.concatenate(parts, axis=0).astype(jnp.bfloat16)


def each_rows(m, step, unroll):
    size = min(unroll * STEP_ROWS, m)

    def run(index, carry):
        for at in range(0, size, STEP_ROWS):
            step(pl.multiple_of(index * size + at, STEP_ROWS))
        return carry

    lax.fori_loop(0, m // size, run, 0)


def depthwise_own_kernel(vol_hbm, kernel_hbm, out_ref, vol_ref, kernel_ref, wide_ref, sems):
    m = vol_ref.shape[0]
    rows = min(BLOCK_ROWS, m)
    core = lax.axis_index("chan") % 2
    lane = lane_index()
    taps_copy = pltpu.make_async_copy(kernel_hbm, kernel_ref, sems.at[0])
    taps_copy.start()
    copies = [
        pltpu.make_async_copy(
            vol_hbm.at[pl.ds(at, rows)], vol_ref.at[pl.ds(at, rows)], sems.at[1 + at // rows]
        )
        for at in range(0, m, rows)
    ]
    for copy in copies:
        copy.start()
    taps_copy.wait()
    spread_taps(kernel_ref, wide_ref)
    for block, copy in enumerate(copies):
        copy.wait()
        for at in range(block * rows, (block + 1) * rows, STEP_ROWS):
            out_ref[at : at + STEP_ROWS, :] = depthwise_rows(vol_ref, wide_ref, at, core, lane)


def depthwise_theirs_kernel(vol_ref, kernel_ref, own_ref, out_ref, wide_ref):
    m = vol_ref.shape[0]
    core = lax.axis_index("chan") % 2
    lane = lane_index()
    spread_taps(kernel_ref, wide_ref)
    out_ref[:m, :] = own_ref[...]

    def step(at):
        out_ref[pl.ds(m + at, STEP_ROWS), :] = depthwise_rows(vol_ref, wide_ref, at, core, lane)

    each_rows(m, step, 2)


VMEM_SPEC = pl.BlockSpec(memory_space=pltpu.VMEM)
HBM_SPEC = pl.BlockSpec(memory_space=pltpu.HBM)


ANY_SPEC = pl.BlockSpec(memory_space=pl.ANY)


def vmem_call(
    kernel, operands, outs, name, scratch=(), alias=None, free=(), hbm=False, out_free=()
):
    if hbm:
        operands = [pltpu.with_memory_space_constraint(x, pltpu.HBM) for x in operands]
    spec = HBM_SPEC if hbm else VMEM_SPEC
    return pl.pallas_call(
        kernel,
        out_shape=outs,
        in_specs=[ANY_SPEC if i in free else spec for i in range(len(operands))],
        out_specs=[HBM_SPEC if i in out_free else VMEM_SPEC for i in range(len(outs))],
        scratch_shapes=list(scratch),
        input_output_aliases=alias or {},
        compiler_params=pltpu.CompilerParams(vmem_limit_bytes=12 * MIB),
        name=name,
    )(*operands)


def held(values):
    return pltpu.with_memory_space_constraint(values, pltpu.HBM)


def position(chips):
    index = lax.axis_index("chan")
    return index % 2, index // 2, place_of(index // 2, chips)


def turn_kernel(mine, theirs, straight, turned):
    m = mine.shape[0]
    straight[:m, :] = mine[...]
    straight[m:, :] = theirs[...]
    turned[:, :m] = mine[...].T
    turned[:, m:] = theirs[...].T


def product(weights, block):
    return jnp.dot(weights, block, preferred_element_type=jnp.float32)


def stash(piece, low, all_ref, owner, core, m):
    high = low + piece.shape[0]
    for half in range(2):
        begin, end = max(low, half * m), min(high, (half + 1) * m)
        if begin >= end:
            continue
        side = core if half == 0 else 1 - core
        at = pl.multiple_of(owner * (2 * m) + side * m + (begin - half * m), STEP_ROWS)
        all_ref[pl.ds(at, end - begin), :] = piece[begin - low : end - low, :]


def assemble_kernel(chips, *refs):
    pieces = refs[: chips - 1]
    straight, total_ref, all_ref = refs[chips - 1 :]
    core, chip, place = position(chips)
    m = pieces[0].shape[0] // 2
    for number, piece in enumerate(pieces):
        distance = (number + 1) // 2
        back = chips - distance if number % 2 == 1 else distance
        owner = chip_at((place + back) % chips, chips)
        stash(piece, 0, all_ref, owner, core, m)
    opposite = chip_at((place + chips // 2) % chips, chips)
    blank = jnp.zeros((2 * m, all_ref.shape[1]), all_ref.dtype)
    all_ref[pl.ds(pl.multiple_of(opposite * (2 * m), 2 * m), 2 * m), :] = blank
    total_ref[...] = product(straight[...], all_ref[...])


def bias_column(ref):
    return jnp.broadcast_to(ref[...].astype(jnp.float32), (GROUP, ref.shape[1])).T[:, 0:1]


def weight_rows(turned, owner, whole):
    return turned[pl.ds(pl.multiple_of(owner * whole, whole), whole), :]


def mix_kernel(
    chips,
    turned,
    right,
    left,
    total_ref,
    bias_mine,
    bias_theirs,
    og_mine,
    og_theirs,
    filled,
    act_mine,
    act_theirs,
    grad_ref,
    all_ref,
    right_ref,
    left_ref,
):
    core, _, place = position(chips)
    m = og_mine.shape[0]
    cut = right.shape[0]
    opposite = chip_at((place + chips // 2) % chips, chips)
    stash(right[...], 0, all_ref, opposite, core, m)
    stash(left[...], cut, all_ref, opposite, core, m)
    block = all_ref[pl.ds(pl.multiple_of(opposite * (2 * m), 2 * m), 2 * m), :]
    sums = total_ref[...] + lax.dot_general(
        weight_rows(turned, opposite, 2 * m),
        block,
        (((0,), (0,)), ((), ())),
        preferred_element_type=jnp.float32,
    )
    here = pl.ds(pl.multiple_of(core * PLANE, PLANE), PLANE)
    for half, (bias_ref, og_ref, act_ref) in enumerate(
        ((bias_mine, og_mine, act_mine), (bias_theirs, og_theirs, act_theirs))
    ):
        rows = slice(half * m, (half + 1) * m)
        pre = sums[rows] + bias_column(bias_ref)
        gate = jax.nn.sigmoid(pre)
        act_ref[...] = (pre * gate).astype(act_ref.dtype)
        grad = og_ref[:, here].astype(jnp.float32) * gate * (1.0 + pre * (1.0 - gate))
        grad_ref[rows, :] = grad.astype(grad_ref.dtype)
    share = product(weight_rows(turned, opposite, 2 * m), grad_ref[...])
    part = right_ref.shape[0]
    right_ref[...] = share[:part].astype(right_ref.dtype)
    left_ref[...] = share[part:].astype(left_ref.dtype)


def pass_kernel(chips, distance, half, turned, grad, came, out_ref):
    _, _, place = position(chips)
    whole = grad.shape[0]
    count = came.shape[0]
    ahead = distance if half == 0 else chips - distance
    owner = chip_at((place + ahead) % chips, chips)
    share = product(weight_rows(turned, owner, whole), grad[...])
    low = 0 if half == 0 else whole - count
    for begin, end in ((0, low), (low, low + count), (low + count, whole)):
        if begin < end:
            part = share[begin:end]
            if begin == low:
                part = part + came[...].astype(jnp.float32)
            out_ref[begin:end, :] = part.astype(out_ref.dtype)


def last_kernel(chips, turned, grad, right, left, made, summed, mine_ref, theirs_ref):
    core, chip, _ = position(chips)
    m = mine_ref.shape[0]
    total = (
        product(weight_rows(turned, chip, 2 * m), grad[...])
        + right[...].astype(jnp.float32)
        + left[...].astype(jnp.float32)
    )
    mine_ref[...] = jnp.where(core == 0, total[:m], total[m:]).astype(mine_ref.dtype)
    theirs_ref[...] = jnp.where(core == 0, total[m:], total[:m]).astype(theirs_ref.dtype)


def join_kernel(mine, theirs, out_ref):
    core = lax.axis_index("chan") % 2
    for ref, plane in ((mine, core), (theirs, 1 - core)):
        out_ref[:, pl.ds(pl.multiple_of(plane * PLANE, PLANE), PLANE)] = ref[...]


LANE_PAIRS = (((1,), (1,)), ((), ()))


def weight_theirs_kernel(grad, all_ref, out_ref, bias_ref):
    m = out_ref.shape[0]
    out_ref[...] = lax.dot_general(
        grad[m:, :], all_ref[...], LANE_PAIRS, preferred_element_type=jnp.float32
    ).astype(out_ref.dtype)
    ones = jnp.ones((GROUP, PLANE), grad.dtype)
    bias_ref[...] = lax.dot_general(
        ones, grad[...], LANE_PAIRS, preferred_element_type=jnp.float32
    )


def weight_mine_kernel(grad, all_ref, came, out_ref):
    m = out_ref.shape[0]
    total = lax.dot_general(
        grad[:m, :], all_ref[...], LANE_PAIRS, preferred_element_type=jnp.float32
    )
    out_ref[...] = (total + came[...].astype(jnp.float32)).astype(out_ref.dtype)


def plane_order(core, chunks, planes):
    planes[core] = chunks[0][...]
    planes[1 - core] = chunks[1][...]


def tap_grad_kernel(together, near_ref, far_ref, vol_ref, spread, *refs):
    if together:
        weight_mine, weight_came, out_ref, weight_out, planes, sums, weight_wide, sems = refs
    else:
        out_ref, planes, sums = refs
    m = vol_ref.shape[0]
    lane = lane_index()
    plane_order(lax.axis_index("chan") % 2, (near_ref, far_ref), planes)

    def weight_copy(number):
        rows = pl.ds(pl.multiple_of(number * STEP_ROWS, STEP_ROWS), STEP_ROWS)
        return pltpu.make_async_copy(weight_wide.at[rows], weight_out.at[rows], sems.at[number])

    def group(at):
        rows = pl.ds(at, STEP_ROWS)
        vol = [
            vol_ref[rows, z * PLANE : (z + 1) * PLANE].astype(jnp.float32) for z in range(DEPTH)
        ]
        grad = [planes[z, rows, :].astype(jnp.float32) for z in range(DEPTH)]
        sum_parts = []
        for low in range(0, STEP_ROWS, GROUP):
            moved_vol = [
                [column_shift(tile_list(vol[z][low : low + GROUP]), c, lane) for c in (-1, 0, 1)]
                for z in range(DEPTH)
            ]
            moved_grad = [
                [row_shift(tile_list(grad[z][low : low + GROUP]), -b, lane) for b in (-1, 0, 1)]
                for z in range(DEPTH)
            ]
            collected = jnp.zeros((GROUP, LANES), jnp.float32)
            for a in (-1, 0, 1):
                for b in range(3):
                    for c in range(3):
                        t = 9 * (a + 1) + 3 * b + c
                        acc = None
                        for z in range(DEPTH):
                            if not 0 <= z + a < DEPTH:
                                continue
                            for left, right in zip(moved_grad[z][b], moved_vol[z + a][c]):
                                acc = left * right if acc is None else acc + left * right
                        collected = jnp.where(
                            lane == t, jnp.sum(acc, axis=1, keepdims=True), collected
                        )
            sum_parts.append(collected)
        sums[rows, :] = jnp.concatenate(sum_parts, axis=0)
        if together:
            weight_wide[rows, :] = weight_mine[rows, :].astype(jnp.float32) + weight_came[
                rows, :
            ].astype(jnp.float32)
            weight_copy(at // STEP_ROWS).start()

    each_rows(m, group, 1)
    out_ref[...] = sums[...].T[:TAPS, :]
    if together:
        for number in range(m // STEP_ROWS):
            weight_copy(number).wait()


def volume_grad_kernel(near_ref, far_ref, wide_ref, out_ref):
    m = out_ref.shape[0]
    core = lax.axis_index("chan") % 2
    lane = lane_index()

    def step(at):
        rows = pl.ds(at, STEP_ROWS)
        grads = [ref[rows, :].astype(jnp.float32) for ref in (near_ref, far_ref)]
        parts = [[], []]
        for low in range(0, STEP_ROWS, GROUP):
            group = pl.ds(at + low, GROUP)
            tiles = [tile_list(values[low : low + GROUP]) for values in grads]
            moved = [[row_shift(plane, 1 - b, lane) for b in range(3)] for plane in tiles]
            for p in range(2):
                columns = [None] * 3
                for c in range(3):
                    for b in range(3):
                        t = 3 * b + c
                        columns[c] = add_tiles(
                            columns[c], [wide_ref[t, group, :] * x for x in moved[p][b]]
                        )
                        u = 9 * (2 - p) + t
                        columns[c] = add_tiles(
                            columns[c], [wide_ref[u, group, :] * x for x in moved[1 - p][b]]
                        )
                shifted = [column_shift(columns[c], 1 - c, lane) for c in (0, 2)]
                total = add_tiles(add_tiles(columns[1], shifted[0]), shifted[1])
                parts[p].append(jnp.concatenate(total, axis=1))
        for p, plane in enumerate((core, 1 - core)):
            place = pl.multiple_of(plane * PLANE, PLANE)
            out_ref[rows, pl.ds(place, PLANE)] = jnp.concatenate(parts[p], axis=0).astype(
                out_ref.dtype
            )

    each_rows(m, step, 1)


def body(volume, depth_kernel, mix_weight, mix_bias, out_grad):
    n = lax.axis_size("chan")
    patches = lax.axis_size("patch")
    chips = n // 2
    half_ring = chips // 2
    core = lax.axis_index("chan") % 2
    m, channels = mix_weight.shape
    whole = 2 * m

    ring = [2 * k if k < half_ring else 2 * (chips - 1 - k) + 1 for k in range(chips)]
    to_core = [(i, i ^ 1) for i in range(n)]
    to_right = [
        (2 * ring[k] + c, 2 * ring[(k + 1) % chips] + c) for k in range(chips) for c in range(2)
    ]
    to_left = [(target, source) for source, target in to_right]

    def shape(rows, columns, kind=jnp.bfloat16):
        return jax.ShapeDtypeStruct((rows, columns), kind)

    def swap(values):
        return lax.ppermute(values, "chan", to_core)

    def send(right, left):
        return lax.ppermute(right, "chan", to_right), lax.ppermute(left, "chan", to_left)

    def over_patches(values):
        if patches != 2:
            return lax.psum(values.astype(jnp.float32), "patch")
        came = lax.ppermute(values, "patch", [(0, 1), (1, 0)])
        return values.astype(jnp.float32) + came.astype(jnp.float32)

    block_rows = min(BLOCK_ROWS, m)
    vol_mine = volume[0]
    vol_theirs = swap(vol_mine)
    kernel_theirs = swap(depth_kernel)
    wide_scratch = pltpu.VMEM((2 * TAPS // 3, m, LANES), jnp.float32)
    (mixed_own,) = vmem_call(
        depthwise_own_kernel,
        (vol_mine, depth_kernel),
        (shape(m, PLANE),),
        "depthwise_own",
        scratch=(
            pltpu.VMEM(vol_mine.shape, jnp.bfloat16),
            pltpu.VMEM(depth_kernel.shape, jnp.bfloat16),
            wide_scratch,
            pltpu.SemaphoreType.DMA((1 + m // block_rows,)),
        ),
        hbm=True,
    )
    (mixed_in,) = vmem_call(
        depthwise_theirs_kernel,
        (vol_theirs, kernel_theirs, mixed_own),
        (shape(whole, PLANE),),
        "depthwise_theirs",
        scratch=(wide_scratch,),
    )

    bias_mine = mix_bias[None, :]
    bias_theirs = swap(bias_mine)
    og_mine = out_grad[0]
    og_theirs = swap(og_mine)
    straight, turned = vmem_call(
        turn_kernel,
        (mix_weight, swap(mix_weight)),
        (shape(whole, channels), shape(channels, whole)),
        "turn",
    )

    (wide_taps,) = vmem_call(
        spread_kernel,
        (depth_kernel,),
        (jax.ShapeDtypeStruct((TAPS, m, LANES), jnp.float32),),
        "spread",
    )

    all_shape = shape(channels, PLANE)
    cut = m
    part = m
    right = left = mixed_in
    pieces = [mixed_in]
    for step in range(1, half_ring):
        right, left = send(right, left)
        pieces += [right, left]
    right, left = send(right[:cut], left[cut:])
    total, all_mixed = vmem_call(
        lambda *refs: assemble_kernel(chips, *refs),
        (*pieces, straight),
        (shape(whole, PLANE, jnp.float32), all_shape),
        "assemble",
    )
    act_mine, act_theirs, pre_grad, all_mixed, right, left = vmem_call(
        lambda *refs: mix_kernel(chips, *refs),
        (
            turned,
            right,
            left,
            total,
            bias_mine,
            bias_theirs,
            og_mine,
            og_theirs,
            all_mixed,
        ),
        (
            shape(m, PLANE),
            shape(m, PLANE),
            shape(whole, PLANE),
            all_shape,
            shape(part, PLANE),
            shape(whole - part, PLANE),
        ),
        "mix",
        alias={8: 3},
    )

    weight_shape = shape(m, channels)
    weight_theirs, bias_part = vmem_call(
        weight_theirs_kernel,
        (pre_grad, all_mixed),
        (weight_shape, shape(GROUP, whole, jnp.float32)),
        "weight_theirs",
    )
    weight_far = swap(weight_theirs)
    bias_grad = over_patches(bias_part[0, :m] + swap(bias_part[0, m:]))
    act_far = swap(act_theirs)
    (weight_sum,) = vmem_call(
        weight_mine_kernel, (pre_grad, all_mixed, weight_far), (weight_shape,), "weight_mine"
    )
    together = patches == 2
    if together:
        weight_came = lax.ppermute(weight_sum, "patch", [(0, 1), (1, 0)])
    else:
        weight_grad = over_patches(weight_sum)
    (activated,) = vmem_call(
        join_kernel, (act_mine, act_far), (shape(m, DEPTH * PLANE),), "join"
    )
    for step in range(1, half_ring):
        right, left = [
            vmem_call(
                lambda *refs, step=step, half=half: pass_kernel(
                    chips, half_ring - step, half, *refs
                ),
                (turned, pre_grad, came),
                (shape(whole, PLANE),),
                "pass",
            )[0]
            for half, came in enumerate(send(right, left))
        ]
    right, left = send(right, left)
    mine, theirs = vmem_call(
        lambda *refs: last_kernel(chips, *refs),
        (turned, pre_grad, right, left, held(activated), held(bias_grad)),
        (shape(m, PLANE),) * 2,
        "last",
        free=(4, 5),
    )
    far = swap(theirs)

    kernel_grad, *made = vmem_call(
        lambda *refs: tap_grad_kernel(together, *refs),
        (mine, far, vol_mine, wide_taps) + ((weight_sum, weight_came) if together else ()),
        (shape(TAPS, m, jnp.float32),)
        + ((shape(m, channels, jnp.float32),) if together else ()),
        "tap_grad",
        scratch=(
            pltpu.VMEM((DEPTH, m, PLANE), jnp.bfloat16),
            pltpu.VMEM((m, LANES), jnp.float32),
        )
        + (
            (
                pltpu.VMEM((m, channels), jnp.float32),
                pltpu.SemaphoreType.DMA((m // STEP_ROWS,)),
            )
            if together
            else ()
        ),
        free=(3,),
        out_free=(1,),
    )
    if together:
        weight_grad = made[0]
    kernel_grad = over_patches(kernel_grad)
    (volume_grad,) = vmem_call(
        volume_grad_kernel,
        (mine, far, wide_taps),
        (shape(m, DEPTH * PLANE),),
        "volume_grad",
    )
    return (
        activated[None],
        volume_grad[None],
        kernel_grad,
        weight_grad,
        bias_grad,
    )


def solution(mesh):
    placed = (
        P("patch", "chan", None),
        P(None, "chan"),
        P("chan", None),
        P("chan"),
        P("patch", "chan", None),
    )
    return jax.shard_map(
        body,
        mesh=mesh,
        in_specs=placed,
        out_specs=(
            P("patch", "chan", None),
            P("patch", "chan", None),
            P(None, "chan"),
            P("chan", None),
            P("chan"),
        ),
        check_vma=False,
    )
```

```python
import jax
import jax.numpy as jnp
from jax import lax
from jax.experimental import pallas as pl
from jax.experimental.pallas import tpu as pltpu
from jax.sharding import PartitionSpec as P

DEPTH = 2
ROWS = 16
SIDE = 32
PLANE = ROWS * SIDE
LANES = 128
VREGS = PLANE // LANES
GROUP = 8
STEP_ROWS = 16
TAPS = 27
TAP_ROWS = 32
BLOCK_ROWS = 32
MIB = 1024 * 1024


def chip_at(place, chips):
    return jnp.where(place < chips // 2, 2 * place, 2 * (chips - 1 - place) + 1)


def place_of(chip, chips):
    return jnp.where(chip % 2 == 0, chip // 2, chips - 1 - chip // 2)


def lane_index():
    return lax.broadcasted_iota(jnp.int32, (GROUP, LANES), 1)


def column_shift(tiles, step, lane):
    if step == 0:
        return tiles
    inside = lane % SIDE != (SIDE - 1 if step > 0 else 0)
    return [
        jnp.where(inside, pltpu.roll(tile, (-step) % LANES, 1), 0.0) for tile in tiles
    ]


def row_shift(tiles, step, lane):
    if step == 0:
        return tiles
    turned = [pltpu.roll(tile, (-step * SIDE) % LANES, 1) for tile in tiles]
    zero = jnp.zeros_like(tiles[0])
    if step > 0:
        ahead = turned[1:] + [zero]
        return [jnp.where(lane < LANES - SIDE, now, far) for now, far in zip(turned, ahead)]
    behind = [zero] + turned[:-1]
    return [jnp.where(lane >= SIDE, now, far) for now, far in zip(turned, behind)]


def tile_list(values):
    return [values[:, LANES * at : LANES * (at + 1)] for at in range(VREGS)]


def add_tiles(left, right):
    return right if left is None else [a + b for a, b in zip(left, right)]


def scale_tiles(column, tiles):
    wide = jnp.broadcast_to(column, (GROUP, LANES))
    return [wide * tile for tile in tiles]


def tap_columns(kernel_ref):
    taps = kernel_ref[...].astype(jnp.float32)
    core = lax.axis_index("chan") % 2
    down, same, up = taps[0:9], taps[9:18], taps[18:27]
    pad = jnp.zeros((TAP_ROWS - TAPS, taps.shape[1]), jnp.float32)
    order = [same, jnp.where(core == 0, up, down), jnp.where(core == 0, down, up), pad]
    return jnp.concatenate(order, axis=0).T


def spread_taps(kernel_ref, wide_ref):
    columns = tap_columns(kernel_ref)
    for t in range(wide_ref.shape[0]):
        wide_ref[t] = jnp.broadcast_to(columns[:, t : t + 1], (columns.shape[0], LANES))


def spread_kernel(kernel_ref, wide_ref):
    spread_taps(kernel_ref, wide_ref)


def depthwise_rows(vol_ref, wide_ref, at, core, lane):
    rows = pl.ds(at, STEP_ROWS)
    sources = [
        vol_ref[rows, pl.ds(pl.multiple_of(plane * PLANE, PLANE), PLANE)].astype(jnp.float32)
        for plane in (core, 1 - core)
    ]
    parts = []
    for low in range(0, STEP_ROWS, GROUP):
        group = pl.ds(at + low, GROUP)
        tiles = [tile_list(values[low : low + GROUP]) for values in sources]
        moved = [[column_shift(plane, c, lane) for c in (-1, 0, 1)] for plane in tiles]
        lines = [None] * 3
        for b in range(3):
            for side in range(2):
                for c in range(3):
                    wide = wide_ref[9 * side + 3 * b + c, group, :]
                    lines[b] = add_tiles(lines[b], [wide * tile for tile in moved[side][c]])
        shifted = [row_shift(lines[b], b - 1, lane) for b in (0, 2)]
        total = add_tiles(add_tiles(lines[1], shifted[0]), shifted[1])
        parts.append(jnp.concatenate(total, axis=1))
    return jnp.concatenate(parts, axis=0).astype(jnp.bfloat16)


def each_rows(m, step, unroll):
    size = min(unroll * STEP_ROWS, m)

    def run(index, carry):
        for at in range(0, size, STEP_ROWS):
            step(pl.multiple_of(index * size + at, STEP_ROWS))
        return carry

    lax.fori_loop(0, m // size, run, 0)


def depthwise_own_kernel(vol_hbm, kernel_hbm, out_ref, vol_ref, kernel_ref, wide_ref, sems):
    m = vol_ref.shape[0]
    rows = min(BLOCK_ROWS, m)
    core = lax.axis_index("chan") % 2
    lane = lane_index()
    taps_copy = pltpu.make_async_copy(kernel_hbm, kernel_ref, sems.at[0])
    taps_copy.start()
    copies = [
        pltpu.make_async_copy(
            vol_hbm.at[pl.ds(at, rows)], vol_ref.at[pl.ds(at, rows)], sems.at[1 + at // rows]
        )
        for at in range(0, m, rows)
    ]
    for copy in copies:
        copy.start()
    taps_copy.wait()
    spread_taps(kernel_ref, wide_ref)
    for block, copy in enumerate(copies):
        copy.wait()
        for at in range(block * rows, (block + 1) * rows, STEP_ROWS):
            out_ref[at : at + STEP_ROWS, :] = depthwise_rows(vol_ref, wide_ref, at, core, lane)


def depthwise_theirs_kernel(vol_ref, kernel_ref, own_ref, out_ref, wide_ref):
    m = vol_ref.shape[0]
    core = lax.axis_index("chan") % 2
    lane = lane_index()
    spread_taps(kernel_ref, wide_ref)
    out_ref[:m, :] = own_ref[...]

    def step(at):
        out_ref[pl.ds(m + at, STEP_ROWS), :] = depthwise_rows(vol_ref, wide_ref, at, core, lane)

    each_rows(m, step, 4)


VMEM_SPEC = pl.BlockSpec(memory_space=pltpu.VMEM)
HBM_SPEC = pl.BlockSpec(memory_space=pltpu.HBM)


ANY_SPEC = pl.BlockSpec(memory_space=pl.ANY)


def vmem_call(
    kernel, operands, outs, name, scratch=(), alias=None, free=(), hbm=False, out_free=()
):
    if hbm:
        operands = [pltpu.with_memory_space_constraint(x, pltpu.HBM) for x in operands]
    spec = HBM_SPEC if hbm else VMEM_SPEC
    return pl.pallas_call(
        kernel,
        out_shape=outs,
        in_specs=[ANY_SPEC if i in free else spec for i in range(len(operands))],
        out_specs=[HBM_SPEC if i in out_free else VMEM_SPEC for i in range(len(outs))],
        scratch_shapes=list(scratch),
        input_output_aliases=alias or {},
        compiler_params=pltpu.CompilerParams(vmem_limit_bytes=12 * MIB),
        name=name,
    )(*operands)


def held(values):
    return pltpu.with_memory_space_constraint(values, pltpu.HBM)


def position(chips):
    index = lax.axis_index("chan")
    return index % 2, index // 2, place_of(index // 2, chips)


def turn_kernel(mine, theirs, straight, turned):
    m = mine.shape[0]
    straight[:m, :] = mine[...]
    straight[m:, :] = theirs[...]
    turned[:, :m] = mine[...].T
    turned[:, m:] = theirs[...].T


def product(weights, block):
    return jnp.dot(weights, block, preferred_element_type=jnp.float32)


def stash(piece, low, all_ref, owner, core, m):
    high = low + piece.shape[0]
    for half in range(2):
        begin, end = max(low, half * m), min(high, (half + 1) * m)
        if begin >= end:
            continue
        side = core if half == 0 else 1 - core
        at = pl.multiple_of(owner * (2 * m) + side * m + (begin - half * m), STEP_ROWS)
        all_ref[pl.ds(at, end - begin), :] = piece[begin - low : end - low, :]


def assemble_kernel(chips, *refs):
    pieces = refs[: chips - 1]
    straight, total_ref, all_ref = refs[chips - 1 :]
    core, chip, place = position(chips)
    m = pieces[0].shape[0] // 2
    for number, piece in enumerate(pieces):
        distance = (number + 1) // 2
        back = chips - distance if number % 2 == 1 else distance
        owner = chip_at((place + back) % chips, chips)
        stash(piece, 0, all_ref, owner, core, m)
    opposite = chip_at((place + chips // 2) % chips, chips)
    blank = jnp.zeros((2 * m, all_ref.shape[1]), all_ref.dtype)
    all_ref[pl.ds(pl.multiple_of(opposite * (2 * m), 2 * m), 2 * m), :] = blank
    total_ref[...] = product(straight[...], all_ref[...])


def bias_column(ref):
    return jnp.broadcast_to(ref[...].astype(jnp.float32), (GROUP, ref.shape[1])).T[:, 0:1]


def weight_rows(turned, owner, whole):
    return turned[pl.ds(pl.multiple_of(owner * whole, whole), whole), :]


def mix_kernel(
    chips,
    turned,
    right,
    left,
    total_ref,
    bias_mine,
    bias_theirs,
    og_mine,
    og_theirs,
    filled,
    act_mine,
    act_theirs,
    grad_ref,
    all_ref,
    right_ref,
    left_ref,
):
    core, _, place = position(chips)
    m = og_mine.shape[0]
    cut = right.shape[0]
    opposite = chip_at((place + chips // 2) % chips, chips)
    stash(right[...], 0, all_ref, opposite, core, m)
    stash(left[...], cut, all_ref, opposite, core, m)
    block = all_ref[pl.ds(pl.multiple_of(opposite * (2 * m), 2 * m), 2 * m), :]
    sums = total_ref[...] + lax.dot_general(
        weight_rows(turned, opposite, 2 * m),
        block,
        (((0,), (0,)), ((), ())),
        preferred_element_type=jnp.float32,
    )
    here = pl.ds(pl.multiple_of(core * PLANE, PLANE), PLANE)
    for half, (bias_ref, og_ref, act_ref) in enumerate(
        ((bias_mine, og_mine, act_mine), (bias_theirs, og_theirs, act_theirs))
    ):
        rows = slice(half * m, (half + 1) * m)
        pre = sums[rows] + bias_column(bias_ref)
        gate = jax.nn.sigmoid(pre)
        act_ref[...] = (pre * gate).astype(act_ref.dtype)
        grad = og_ref[:, here].astype(jnp.float32) * gate * (1.0 + pre * (1.0 - gate))
        grad_ref[rows, :] = grad.astype(grad_ref.dtype)
    share = product(weight_rows(turned, opposite, 2 * m), grad_ref[...])
    part = right_ref.shape[0]
    right_ref[...] = share[:part].astype(right_ref.dtype)
    left_ref[...] = share[part:].astype(left_ref.dtype)


def pass_kernel(chips, distance, half, turned, grad, came, out_ref):
    _, _, place = position(chips)
    whole = grad.shape[0]
    count = came.shape[0]
    ahead = distance if half == 0 else chips - distance
    owner = chip_at((place + ahead) % chips, chips)
    share = product(weight_rows(turned, owner, whole), grad[...])
    low = 0 if half == 0 else whole - count
    for begin, end in ((0, low), (low, low + count), (low + count, whole)):
        if begin < end:
            part = share[begin:end]
            if begin == low:
                part = part + came[...].astype(jnp.float32)
            out_ref[begin:end, :] = part.astype(out_ref.dtype)


def last_kernel(chips, turned, grad, right, left, made, summed, mine_ref, theirs_ref):
    core, chip, _ = position(chips)
    m = mine_ref.shape[0]
    total = (
        product(weight_rows(turned, chip, 2 * m), grad[...])
        + right[...].astype(jnp.float32)
        + left[...].astype(jnp.float32)
    )
    mine_ref[...] = jnp.where(core == 0, total[:m], total[m:]).astype(mine_ref.dtype)
    theirs_ref[...] = jnp.where(core == 0, total[m:], total[:m]).astype(theirs_ref.dtype)


def join_kernel(mine, theirs, out_ref):
    core = lax.axis_index("chan") % 2
    for ref, plane in ((mine, core), (theirs, 1 - core)):
        out_ref[:, pl.ds(pl.multiple_of(plane * PLANE, PLANE), PLANE)] = ref[...]


LANE_PAIRS = (((1,), (1,)), ((), ()))


def weight_theirs_kernel(grad, all_ref, out_ref, bias_ref):
    m = out_ref.shape[0]
    out_ref[...] = lax.dot_general(
        grad[m:, :], all_ref[...], LANE_PAIRS, preferred_element_type=jnp.float32
    ).astype(out_ref.dtype)
    ones = jnp.ones((GROUP, PLANE), grad.dtype)
    bias_ref[...] = lax.dot_general(
        ones, grad[...], LANE_PAIRS, preferred_element_type=jnp.float32
    )


def weight_mine_kernel(grad, all_ref, came, out_ref):
    m = out_ref.shape[0]
    total = lax.dot_general(
        grad[:m, :], all_ref[...], LANE_PAIRS, preferred_element_type=jnp.float32
    )
    out_ref[...] = (total + came[...].astype(jnp.float32)).astype(out_ref.dtype)


def plane_order(core, chunks, planes):
    planes[core] = chunks[0][...]
    planes[1 - core] = chunks[1][...]


def tap_grad_kernel(near_ref, far_ref, vol_ref, spread, out_ref, planes, sums):
    m = vol_ref.shape[0]
    lane = lane_index()
    plane_order(lax.axis_index("chan") % 2, (near_ref, far_ref), planes)

    def group(at):
        rows = pl.ds(at, STEP_ROWS)
        vol = [
            vol_ref[rows, z * PLANE : (z + 1) * PLANE].astype(jnp.float32) for z in range(DEPTH)
        ]
        grad = [planes[z, rows, :].astype(jnp.float32) for z in range(DEPTH)]
        sum_parts = []
        for low in range(0, STEP_ROWS, GROUP):
            moved_vol = [
                [column_shift(tile_list(vol[z][low : low + GROUP]), c, lane) for c in (-1, 0, 1)]
                for z in range(DEPTH)
            ]
            moved_grad = [
                [row_shift(tile_list(grad[z][low : low + GROUP]), -b, lane) for b in (-1, 0, 1)]
                for z in range(DEPTH)
            ]
            collected = jnp.zeros((GROUP, LANES), jnp.float32)
            for a in (-1, 0, 1):
                for b in range(3):
                    for c in range(3):
                        t = 9 * (a + 1) + 3 * b + c
                        acc = None
                        for z in range(DEPTH):
                            if not 0 <= z + a < DEPTH:
                                continue
                            for left, right in zip(moved_grad[z][b], moved_vol[z + a][c]):
                                acc = left * right if acc is None else acc + left * right
                        collected = jnp.where(
                            lane == t, jnp.sum(acc, axis=1, keepdims=True), collected
                        )
            sum_parts.append(collected)
        sums[rows, :] = jnp.concatenate(sum_parts, axis=0)

    each_rows(m, group, 1)
    out_ref[...] = sums[...].T[:TAPS, :]

def volume_grad_kernel(together, near_ref, far_ref, wide_ref, *refs):
    if together:
        weight_mine, weight_came, out_ref, weight_out, weight_wide, sems = refs
    else:
        (out_ref,) = refs
    m = out_ref.shape[0]
    core = lax.axis_index("chan") % 2
    lane = lane_index()

    def weight_copy(number):
        rows = pl.ds(pl.multiple_of(number * STEP_ROWS, STEP_ROWS), STEP_ROWS)
        return pltpu.make_async_copy(weight_wide.at[rows], weight_out.at[rows], sems.at[number])

    def step(at):
        rows = pl.ds(at, STEP_ROWS)
        grads = [ref[rows, :].astype(jnp.float32) for ref in (near_ref, far_ref)]
        parts = [[], []]
        for low in range(0, STEP_ROWS, GROUP):
            group = pl.ds(at + low, GROUP)
            tiles = [tile_list(values[low : low + GROUP]) for values in grads]
            moved = [[row_shift(plane, 1 - b, lane) for b in range(3)] for plane in tiles]
            for p in range(2):
                columns = [None] * 3
                for c in range(3):
                    for b in range(3):
                        t = 3 * b + c
                        columns[c] = add_tiles(
                            columns[c], [wide_ref[t, group, :] * x for x in moved[p][b]]
                        )
                        u = 9 * (2 - p) + t
                        columns[c] = add_tiles(
                            columns[c], [wide_ref[u, group, :] * x for x in moved[1 - p][b]]
                        )
                shifted = [column_shift(columns[c], 1 - c, lane) for c in (0, 2)]
                total = add_tiles(add_tiles(columns[1], shifted[0]), shifted[1])
                parts[p].append(jnp.concatenate(total, axis=1))
        for p, plane in enumerate((core, 1 - core)):
            place = pl.multiple_of(plane * PLANE, PLANE)
            out_ref[rows, pl.ds(place, PLANE)] = jnp.concatenate(parts[p], axis=0).astype(
                out_ref.dtype
            )

        if together:
            weight_wide[rows, :] = weight_mine[rows, :].astype(jnp.float32) + weight_came[
                rows, :
            ].astype(jnp.float32)
            weight_copy(at // STEP_ROWS).start()

    each_rows(m, step, 2)
    if together:
        for number in range(m // STEP_ROWS):
            weight_copy(number).wait()


def body(volume, depth_kernel, mix_weight, mix_bias, out_grad):
    n = lax.axis_size("chan")
    patches = lax.axis_size("patch")
    chips = n // 2
    half_ring = chips // 2
    core = lax.axis_index("chan") % 2
    m, channels = mix_weight.shape
    whole = 2 * m

    ring = [2 * k if k < half_ring else 2 * (chips - 1 - k) + 1 for k in range(chips)]
    to_core = [(i, i ^ 1) for i in range(n)]
    to_right = [
        (2 * ring[k] + c, 2 * ring[(k + 1) % chips] + c) for k in range(chips) for c in range(2)
    ]
    to_left = [(target, source) for source, target in to_right]

    def shape(rows, columns, kind=jnp.bfloat16):
        return jax.ShapeDtypeStruct((rows, columns), kind)

    def swap(values):
        return lax.ppermute(values, "chan", to_core)

    def send(right, left):
        return lax.ppermute(right, "chan", to_right), lax.ppermute(left, "chan", to_left)

    def over_patches(values):
        if patches != 2:
            return lax.psum(values.astype(jnp.float32), "patch")
        came = lax.ppermute(values, "patch", [(0, 1), (1, 0)])
        return values.astype(jnp.float32) + came.astype(jnp.float32)

    block_rows = min(BLOCK_ROWS, m)
    vol_mine = volume[0]
    vol_theirs = swap(vol_mine)
    kernel_theirs = swap(depth_kernel)
    wide_scratch = pltpu.VMEM((2 * TAPS // 3, m, LANES), jnp.float32)
    (mixed_own,) = vmem_call(
        depthwise_own_kernel,
        (vol_mine, depth_kernel),
        (shape(m, PLANE),),
        "depthwise_own",
        scratch=(
            pltpu.VMEM(vol_mine.shape, jnp.bfloat16),
            pltpu.VMEM(depth_kernel.shape, jnp.bfloat16),
            wide_scratch,
            pltpu.SemaphoreType.DMA((1 + m // block_rows,)),
        ),
        hbm=True,
    )
    (mixed_in,) = vmem_call(
        depthwise_theirs_kernel,
        (vol_theirs, kernel_theirs, mixed_own),
        (shape(whole, PLANE),),
        "depthwise_theirs",
        scratch=(wide_scratch,),
    )

    bias_mine = mix_bias[None, :]
    bias_theirs = swap(bias_mine)
    og_mine = out_grad[0]
    og_theirs = swap(og_mine)
    straight, turned = vmem_call(
        turn_kernel,
        (mix_weight, swap(mix_weight)),
        (shape(whole, channels), shape(channels, whole)),
        "turn",
    )

    (wide_taps,) = vmem_call(
        spread_kernel,
        (depth_kernel,),
        (jax.ShapeDtypeStruct((TAPS, m, LANES), jnp.float32),),
        "spread",
    )

    all_shape = shape(channels, PLANE)
    cut = m
    part = m
    right = left = mixed_in
    pieces = [mixed_in]
    for step in range(1, half_ring):
        right, left = send(right, left)
        pieces += [right, left]
    right, left = send(right[:cut], left[cut:])
    total, all_mixed = vmem_call(
        lambda *refs: assemble_kernel(chips, *refs),
        (*pieces, straight),
        (shape(whole, PLANE, jnp.float32), all_shape),
        "assemble",
    )
    act_mine, act_theirs, pre_grad, all_mixed, right, left = vmem_call(
        lambda *refs: mix_kernel(chips, *refs),
        (
            turned,
            right,
            left,
            total,
            bias_mine,
            bias_theirs,
            og_mine,
            og_theirs,
            all_mixed,
        ),
        (
            shape(m, PLANE),
            shape(m, PLANE),
            shape(whole, PLANE),
            all_shape,
            shape(part, PLANE),
            shape(whole - part, PLANE),
        ),
        "mix",
        alias={8: 3},
    )

    weight_shape = shape(m, channels)
    weight_theirs, bias_part = vmem_call(
        weight_theirs_kernel,
        (pre_grad, all_mixed),
        (weight_shape, shape(GROUP, whole, jnp.float32)),
        "weight_theirs",
    )
    weight_far = swap(weight_theirs)
    bias_grad = over_patches(bias_part[0, :m] + swap(bias_part[0, m:]))
    act_far = swap(act_theirs)
    (weight_sum,) = vmem_call(
        weight_mine_kernel, (pre_grad, all_mixed, weight_far), (weight_shape,), "weight_mine"
    )
    together = patches == 2
    if together:
        weight_came = lax.ppermute(weight_sum, "patch", [(0, 1), (1, 0)])
    else:
        weight_grad = over_patches(weight_sum)
    (activated,) = vmem_call(
        join_kernel, (act_mine, act_far), (shape(m, DEPTH * PLANE),), "join"
    )
    for step in range(1, half_ring):
        right, left = [
            vmem_call(
                lambda *refs, step=step, half=half: pass_kernel(
                    chips, half_ring - step, half, *refs
                ),
                (turned, pre_grad, came),
                (shape(whole, PLANE),),
                "pass",
            )[0]
            for half, came in enumerate(send(right, left))
        ]
    right, left = send(right, left)
    mine, theirs = vmem_call(
        lambda *refs: last_kernel(chips, *refs),
        (turned, pre_grad, right, left, held(activated), held(bias_grad)),
        (shape(m, PLANE),) * 2,
        "last",
        free=(4, 5),
    )
    far = swap(theirs)

    (kernel_grad,) = vmem_call(
        tap_grad_kernel,
        (mine, far, vol_mine, wide_taps),
        (shape(TAPS, m, jnp.float32),),
        "tap_grad",
        scratch=(
            pltpu.VMEM((DEPTH, m, PLANE), jnp.bfloat16),
            pltpu.VMEM((m, LANES), jnp.float32),
        ),
        free=(3,),
    )
    kernel_grad = over_patches(kernel_grad)
    weights, weight_outs, weight_scratch = (), (), ()
    if together:
        weights = (weight_sum, weight_came)
        weight_outs = (shape(m, channels, jnp.float32),)
        weight_scratch = (
            pltpu.VMEM((m, channels), jnp.float32),
            pltpu.SemaphoreType.DMA((m // STEP_ROWS,)),
        )
    volume_grad, *weight_made = vmem_call(
        lambda *refs: volume_grad_kernel(together, *refs),
        (mine, far, wide_taps, *weights),
        (shape(m, DEPTH * PLANE), *weight_outs),
        "volume_grad",
        scratch=weight_scratch,
        out_free=(1,),
    )
    if together:
        (weight_grad,) = weight_made
    return (
        activated[None],
        volume_grad[None],
        kernel_grad,
        weight_grad,
        bias_grad,
    )


def solution(mesh):
    placed = (
        P("patch", "chan", None),
        P(None, "chan"),
        P("chan", None),
        P("chan"),
        P("patch", "chan", None),
    )
    return jax.shard_map(
        body,
        mesh=mesh,
        in_specs=placed,
        out_specs=(
            P("patch", "chan", None),
            P("patch", "chan", None),
            P(None, "chan"),
            P("chan", None),
            P("chan"),
        ),
        check_vma=False,
    )
```

```python
import jax
import jax.numpy as jnp
from jax import lax
from jax.experimental import pallas as pl
from jax.experimental.pallas import tpu as pltpu
from jax.sharding import PartitionSpec as P

DEPTH = 2
ROWS = 16
SIDE = 32
PLANE = ROWS * SIDE
LANES = 128
VREGS = PLANE // LANES
GROUP = 8
STEP_ROWS = 16
TAPS = 27
TAP_ROWS = 32
BLOCK_ROWS = 64
MIB = 1024 * 1024


def chip_at(place, chips):
    return jnp.where(place < chips // 2, 2 * place, 2 * (chips - 1 - place) + 1)


def place_of(chip, chips):
    return jnp.where(chip % 2 == 0, chip // 2, chips - 1 - chip // 2)


def lane_index():
    return lax.broadcasted_iota(jnp.int32, (GROUP, LANES), 1)


def column_shift(tiles, step, lane):
    if step == 0:
        return tiles
    inside = lane % SIDE != (SIDE - 1 if step > 0 else 0)
    return [
        jnp.where(inside, pltpu.roll(tile, (-step) % LANES, 1), 0.0) for tile in tiles
    ]


def row_shift(tiles, step, lane):
    if step == 0:
        return tiles
    turned = [pltpu.roll(tile, (-step * SIDE) % LANES, 1) for tile in tiles]
    zero = jnp.zeros_like(tiles[0])
    if step > 0:
        ahead = turned[1:] + [zero]
        return [jnp.where(lane < LANES - SIDE, now, far) for now, far in zip(turned, ahead)]
    behind = [zero] + turned[:-1]
    return [jnp.where(lane >= SIDE, now, far) for now, far in zip(turned, behind)]


def tile_list(values):
    return [values[:, LANES * at : LANES * (at + 1)] for at in range(VREGS)]


def add_tiles(left, right):
    return right if left is None else [a + b for a, b in zip(left, right)]


def scale_tiles(column, tiles):
    wide = jnp.broadcast_to(column, (GROUP, LANES))
    return [wide * tile for tile in tiles]


def tap_columns(kernel_ref):
    taps = kernel_ref[...].astype(jnp.float32)
    core = lax.axis_index("chan") % 2
    down, same, up = taps[0:9], taps[9:18], taps[18:27]
    pad = jnp.zeros((TAP_ROWS - TAPS, taps.shape[1]), jnp.float32)
    order = [same, jnp.where(core == 0, up, down), jnp.where(core == 0, down, up), pad]
    return jnp.concatenate(order, axis=0).T


def spread_taps(kernel_ref, wide_ref):
    columns = tap_columns(kernel_ref)
    for t in range(wide_ref.shape[0]):
        wide_ref[t] = jnp.broadcast_to(columns[:, t : t + 1], (columns.shape[0], LANES))


def spread_kernel(kernel_ref, wide_ref):
    spread_taps(kernel_ref, wide_ref)


def depthwise_rows(vol_ref, wide_ref, at, core, lane):
    rows = pl.ds(at, STEP_ROWS)
    sources = [
        vol_ref[rows, pl.ds(pl.multiple_of(plane * PLANE, PLANE), PLANE)].astype(jnp.float32)
        for plane in (core, 1 - core)
    ]
    parts = []
    for low in range(0, STEP_ROWS, GROUP):
        group = pl.ds(at + low, GROUP)
        tiles = [tile_list(values[low : low + GROUP]) for values in sources]
        moved = [[column_shift(plane, c, lane) for c in (-1, 0, 1)] for plane in tiles]
        lines = [None] * 3
        for b in range(3):
            for side in range(2):
                for c in range(3):
                    wide = wide_ref[9 * side + 3 * b + c, group, :]
                    lines[b] = add_tiles(lines[b], [wide * tile for tile in moved[side][c]])
        shifted = [row_shift(lines[b], b - 1, lane) for b in (0, 2)]
        total = add_tiles(add_tiles(lines[1], shifted[0]), shifted[1])
        parts.append(jnp.concatenate(total, axis=1))
    return jnp.concatenate(parts, axis=0).astype(jnp.bfloat16)


def each_rows(m, step, unroll):
    size = min(unroll * STEP_ROWS, m)

    def run(index, carry):
        for at in range(0, size, STEP_ROWS):
            step(pl.multiple_of(index * size + at, STEP_ROWS))
        return carry

    lax.fori_loop(0, m // size, run, 0)


def depthwise_own_kernel(vol_hbm, kernel_hbm, out_ref, vol_ref, kernel_ref, wide_ref, sems):
    m = vol_ref.shape[0]
    rows = min(BLOCK_ROWS, m)
    core = lax.axis_index("chan") % 2
    lane = lane_index()
    taps_copy = pltpu.make_async_copy(kernel_hbm, kernel_ref, sems.at[0])
    taps_copy.start()
    copies = [
        pltpu.make_async_copy(
            vol_hbm.at[pl.ds(at, rows)], vol_ref.at[pl.ds(at, rows)], sems.at[1 + at // rows]
        )
        for at in range(0, m, rows)
    ]
    for copy in copies:
        copy.start()
    taps_copy.wait()
    spread_taps(kernel_ref, wide_ref)
    for block, copy in enumerate(copies):
        copy.wait()
        for at in range(block * rows, (block + 1) * rows, STEP_ROWS):
            out_ref[at : at + STEP_ROWS, :] = depthwise_rows(vol_ref, wide_ref, at, core, lane)


def depthwise_theirs_kernel(vol_ref, kernel_ref, own_ref, out_ref, wide_ref):
    m = vol_ref.shape[0]
    core = lax.axis_index("chan") % 2
    lane = lane_index()
    spread_taps(kernel_ref, wide_ref)
    out_ref[:m, :] = own_ref[...]

    def step(at):
        out_ref[pl.ds(m + at, STEP_ROWS), :] = depthwise_rows(vol_ref, wide_ref, at, core, lane)

    each_rows(m, step, 4)


VMEM_SPEC = pl.BlockSpec(memory_space=pltpu.VMEM)
HBM_SPEC = pl.BlockSpec(memory_space=pltpu.HBM)


ANY_SPEC = pl.BlockSpec(memory_space=pl.ANY)


def vmem_call(
    kernel, operands, outs, name, scratch=(), alias=None, free=(), hbm=False, out_free=()
):
    if hbm:
        operands = [pltpu.with_memory_space_constraint(x, pltpu.HBM) for x in operands]
    spec = HBM_SPEC if hbm else VMEM_SPEC
    return pl.pallas_call(
        kernel,
        out_shape=outs,
        in_specs=[ANY_SPEC if i in free else spec for i in range(len(operands))],
        out_specs=[HBM_SPEC if i in out_free else VMEM_SPEC for i in range(len(outs))],
        scratch_shapes=list(scratch),
        input_output_aliases=alias or {},
        compiler_params=pltpu.CompilerParams(vmem_limit_bytes=12 * MIB),
        name=name,
    )(*operands)


def held(values):
    return pltpu.with_memory_space_constraint(values, pltpu.HBM)


def position(chips):
    index = lax.axis_index("chan")
    return index % 2, index // 2, place_of(index // 2, chips)


def turn_kernel(mine, theirs, straight, turned):
    m = mine.shape[0]
    straight[:m, :] = mine[...]
    straight[m:, :] = theirs[...]
    turned[:, :m] = mine[...].T
    turned[:, m:] = theirs[...].T


def product(weights, block):
    return jnp.dot(weights, block, preferred_element_type=jnp.float32)


def stash(piece, low, all_ref, owner, core, m):
    high = low + piece.shape[0]
    for half in range(2):
        begin, end = max(low, half * m), min(high, (half + 1) * m)
        if begin >= end:
            continue
        side = core if half == 0 else 1 - core
        at = pl.multiple_of(owner * (2 * m) + side * m + (begin - half * m), STEP_ROWS)
        all_ref[pl.ds(at, end - begin), :] = piece[begin - low : end - low, :]


def assemble_kernel(chips, *refs):
    pieces = refs[: chips - 1]
    straight, total_ref, all_ref = refs[chips - 1 :]
    core, chip, place = position(chips)
    m = pieces[0].shape[0] // 2
    for number, piece in enumerate(pieces):
        distance = (number + 1) // 2
        back = chips - distance if number % 2 == 1 else distance
        owner = chip_at((place + back) % chips, chips)
        stash(piece, 0, all_ref, owner, core, m)
    opposite = chip_at((place + chips // 2) % chips, chips)
    blank = jnp.zeros((2 * m, all_ref.shape[1]), all_ref.dtype)
    all_ref[pl.ds(pl.multiple_of(opposite * (2 * m), 2 * m), 2 * m), :] = blank
    total_ref[...] = product(straight[...], all_ref[...])


def bias_column(ref):
    return jnp.broadcast_to(ref[...].astype(jnp.float32), (GROUP, ref.shape[1])).T[:, 0:1]


def weight_rows(turned, owner, whole):
    return turned[pl.ds(pl.multiple_of(owner * whole, whole), whole), :]


def mix_kernel(
    chips,
    turned,
    right,
    left,
    total_ref,
    bias_mine,
    bias_theirs,
    og_mine,
    og_theirs,
    filled,
    act_mine,
    act_theirs,
    grad_ref,
    all_ref,
    right_ref,
    left_ref,
):
    core, _, place = position(chips)
    m = og_mine.shape[0]
    cut = right.shape[0]
    opposite = chip_at((place + chips // 2) % chips, chips)
    stash(right[...], 0, all_ref, opposite, core, m)
    stash(left[...], cut, all_ref, opposite, core, m)
    block = all_ref[pl.ds(pl.multiple_of(opposite * (2 * m), 2 * m), 2 * m), :]
    sums = total_ref[...] + lax.dot_general(
        weight_rows(turned, opposite, 2 * m),
        block,
        (((0,), (0,)), ((), ())),
        preferred_element_type=jnp.float32,
    )
    here = pl.ds(pl.multiple_of(core * PLANE, PLANE), PLANE)
    for half, (bias_ref, og_ref, act_ref) in enumerate(
        ((bias_mine, og_mine, act_mine), (bias_theirs, og_theirs, act_theirs))
    ):
        rows = slice(half * m, (half + 1) * m)
        pre = sums[rows] + bias_column(bias_ref)
        gate = jax.nn.sigmoid(pre)
        act_ref[...] = (pre * gate).astype(act_ref.dtype)
        grad = og_ref[:, here].astype(jnp.float32) * gate * (1.0 + pre * (1.0 - gate))
        grad_ref[rows, :] = grad.astype(grad_ref.dtype)
    share = product(weight_rows(turned, opposite, 2 * m), grad_ref[...])
    part = right_ref.shape[0]
    right_ref[...] = share[:part].astype(right_ref.dtype)
    left_ref[...] = share[part:].astype(left_ref.dtype)


def pass_kernel(chips, distance, half, turned, grad, came, out_ref):
    _, _, place = position(chips)
    whole = grad.shape[0]
    count = came.shape[0]
    ahead = distance if half == 0 else chips - distance
    owner = chip_at((place + ahead) % chips, chips)
    share = product(weight_rows(turned, owner, whole), grad[...])
    low = 0 if half == 0 else whole - count
    for begin, end in ((0, low), (low, low + count), (low + count, whole)):
        if begin < end:
            part = share[begin:end]
            if begin == low:
                part = part + came[...].astype(jnp.float32)
            out_ref[begin:end, :] = part.astype(out_ref.dtype)


def last_kernel(chips, turned, grad, right, left, made, mine_ref, theirs_ref):
    core, chip, _ = position(chips)
    m = mine_ref.shape[0]
    total = (
        product(weight_rows(turned, chip, 2 * m), grad[...])
        + right[...].astype(jnp.float32)
        + left[...].astype(jnp.float32)
    )
    mine_ref[...] = jnp.where(core == 0, total[:m], total[m:]).astype(mine_ref.dtype)
    theirs_ref[...] = jnp.where(core == 0, total[m:], total[:m]).astype(theirs_ref.dtype)


def join_kernel(mine, theirs, out_ref):
    core = lax.axis_index("chan") % 2
    for ref, plane in ((mine, core), (theirs, 1 - core)):
        out_ref[:, pl.ds(pl.multiple_of(plane * PLANE, PLANE), PLANE)] = ref[...]


LANE_PAIRS = (((1,), (1,)), ((), ()))


def weight_theirs_kernel(grad, all_ref, out_ref, bias_ref):
    m = out_ref.shape[0]
    out_ref[...] = lax.dot_general(
        grad[m:, :], all_ref[...], LANE_PAIRS, preferred_element_type=jnp.float32
    ).astype(out_ref.dtype)
    ones = jnp.ones((GROUP, PLANE), grad.dtype)
    bias_ref[...] = lax.dot_general(
        ones, grad[...], LANE_PAIRS, preferred_element_type=jnp.float32
    )


def weight_mine_kernel(grad, all_ref, came, out_ref):
    m = out_ref.shape[0]
    total = lax.dot_general(
        grad[:m, :], all_ref[...], LANE_PAIRS, preferred_element_type=jnp.float32
    )
    out_ref[...] = (total + came[...].astype(jnp.float32)).astype(out_ref.dtype)


def plane_order(core, chunks, planes):
    planes[core] = chunks[0][...]
    planes[1 - core] = chunks[1][...]


def tap_grad_kernel(
    near_ref, far_ref, vol_ref, spread, bias_ref, bias_far, out_ref, planes, sums
):
    m = vol_ref.shape[0]
    lane = lane_index()
    plane_order(lax.axis_index("chan") % 2, (near_ref, far_ref), planes)

    def group(at):
        rows = pl.ds(at, STEP_ROWS)
        vol = [
            vol_ref[rows, z * PLANE : (z + 1) * PLANE].astype(jnp.float32) for z in range(DEPTH)
        ]
        grad = [planes[z, rows, :].astype(jnp.float32) for z in range(DEPTH)]
        sum_parts = []
        for low in range(0, STEP_ROWS, GROUP):
            moved_vol = [
                [column_shift(tile_list(vol[z][low : low + GROUP]), c, lane) for c in (-1, 0, 1)]
                for z in range(DEPTH)
            ]
            moved_grad = [
                [row_shift(tile_list(grad[z][low : low + GROUP]), -b, lane) for b in (-1, 0, 1)]
                for z in range(DEPTH)
            ]
            collected = jnp.zeros((GROUP, LANES), jnp.float32)
            for a in (-1, 0, 1):
                for b in range(3):
                    for c in range(3):
                        t = 9 * (a + 1) + 3 * b + c
                        acc = None
                        for z in range(DEPTH):
                            if not 0 <= z + a < DEPTH:
                                continue
                            for left, right in zip(moved_grad[z][b], moved_vol[z + a][c]):
                                acc = left * right if acc is None else acc + left * right
                        collected = jnp.where(
                            lane == t, jnp.sum(acc, axis=1, keepdims=True), collected
                        )
            sum_parts.append(collected)
        sums[rows, :] = jnp.concatenate(sum_parts, axis=0)

    each_rows(m, group, 1)
    out_ref[:TAPS, :] = sums[...].T[:TAPS, :]
    out_ref[TAPS : TAPS + 1, :] = bias_ref[0:1, :m] + bias_far[0:1, :]

def volume_grad_kernel(together, near_ref, far_ref, wide_ref, *refs):
    if together:
        weight_mine, weight_came, out_ref, weight_out, weight_wide, sems = refs
    else:
        (out_ref,) = refs
    m = out_ref.shape[0]
    core = lax.axis_index("chan") % 2
    lane = lane_index()

    def weight_copy(number):
        rows = pl.ds(pl.multiple_of(number * STEP_ROWS, STEP_ROWS), STEP_ROWS)
        return pltpu.make_async_copy(weight_wide.at[rows], weight_out.at[rows], sems.at[number])

    def step(at):
        rows = pl.ds(at, STEP_ROWS)
        grads = [ref[rows, :].astype(jnp.float32) for ref in (near_ref, far_ref)]
        parts = [[], []]
        for low in range(0, STEP_ROWS, GROUP):
            group = pl.ds(at + low, GROUP)
            tiles = [tile_list(values[low : low + GROUP]) for values in grads]
            moved = [[row_shift(plane, 1 - b, lane) for b in range(3)] for plane in tiles]
            for p in range(2):
                columns = [None] * 3
                for c in range(3):
                    for b in range(3):
                        t = 3 * b + c
                        columns[c] = add_tiles(
                            columns[c], [wide_ref[t, group, :] * x for x in moved[p][b]]
                        )
                        u = 9 * (2 - p) + t
                        columns[c] = add_tiles(
                            columns[c], [wide_ref[u, group, :] * x for x in moved[1 - p][b]]
                        )
                shifted = [column_shift(columns[c], 1 - c, lane) for c in (0, 2)]
                total = add_tiles(add_tiles(columns[1], shifted[0]), shifted[1])
                parts[p].append(jnp.concatenate(total, axis=1))
        for p, plane in enumerate((core, 1 - core)):
            place = pl.multiple_of(plane * PLANE, PLANE)
            out_ref[rows, pl.ds(place, PLANE)] = jnp.concatenate(parts[p], axis=0).astype(
                out_ref.dtype
            )

        if together:
            weight_wide[rows, :] = weight_mine[rows, :].astype(jnp.float32) + weight_came[
                rows, :
            ].astype(jnp.float32)
            weight_copy(at // STEP_ROWS).start()

    each_rows(m, step, 2)
    if together:
        for number in range(m // STEP_ROWS):
            weight_copy(number).wait()


def body(volume, depth_kernel, mix_weight, mix_bias, out_grad):
    n = lax.axis_size("chan")
    patches = lax.axis_size("patch")
    chips = n // 2
    half_ring = chips // 2
    core = lax.axis_index("chan") % 2
    m, channels = mix_weight.shape
    whole = 2 * m

    ring = [2 * k if k < half_ring else 2 * (chips - 1 - k) + 1 for k in range(chips)]
    to_core = [(i, i ^ 1) for i in range(n)]
    to_right = [
        (2 * ring[k] + c, 2 * ring[(k + 1) % chips] + c) for k in range(chips) for c in range(2)
    ]
    to_left = [(target, source) for source, target in to_right]

    def shape(rows, columns, kind=jnp.bfloat16):
        return jax.ShapeDtypeStruct((rows, columns), kind)

    def swap(values):
        return lax.ppermute(values, "chan", to_core)

    def send(right, left):
        return lax.ppermute(right, "chan", to_right), lax.ppermute(left, "chan", to_left)

    def over_patches(values):
        if patches != 2:
            return lax.psum(values.astype(jnp.float32), "patch")
        came = lax.ppermute(values, "patch", [(0, 1), (1, 0)])
        return values.astype(jnp.float32) + came.astype(jnp.float32)

    block_rows = min(BLOCK_ROWS, m)
    vol_mine = volume[0]
    vol_theirs = swap(vol_mine)
    kernel_theirs = swap(depth_kernel)
    wide_scratch = pltpu.VMEM((2 * TAPS // 3, m, LANES), jnp.float32)
    (mixed_own,) = vmem_call(
        depthwise_own_kernel,
        (vol_mine, depth_kernel),
        (shape(m, PLANE),),
        "depthwise_own",
        scratch=(
            pltpu.VMEM(vol_mine.shape, jnp.bfloat16),
            pltpu.VMEM(depth_kernel.shape, jnp.bfloat16),
            wide_scratch,
            pltpu.SemaphoreType.DMA((1 + m // block_rows,)),
        ),
        hbm=True,
    )
    (mixed_in,) = vmem_call(
        depthwise_theirs_kernel,
        (vol_theirs, kernel_theirs, mixed_own),
        (shape(whole, PLANE),),
        "depthwise_theirs",
        scratch=(wide_scratch,),
    )

    bias_mine = mix_bias[None, :]
    bias_theirs = swap(bias_mine)
    og_mine = out_grad[0]
    og_theirs = swap(og_mine)
    straight, turned = vmem_call(
        turn_kernel,
        (mix_weight, swap(mix_weight)),
        (shape(whole, channels), shape(channels, whole)),
        "turn",
    )

    (wide_taps,) = vmem_call(
        spread_kernel,
        (depth_kernel,),
        (jax.ShapeDtypeStruct((TAPS, m, LANES), jnp.float32),),
        "spread",
    )

    all_shape = shape(channels, PLANE)
    cut = m
    part = m
    right = left = mixed_in
    pieces = [mixed_in]
    for step in range(1, half_ring):
        right, left = send(right, left)
        pieces += [right, left]
    right, left = send(right[:cut], left[cut:])
    total, all_mixed = vmem_call(
        lambda *refs: assemble_kernel(chips, *refs),
        (*pieces, straight),
        (shape(whole, PLANE, jnp.float32), all_shape),
        "assemble",
    )
    act_mine, act_theirs, pre_grad, all_mixed, right, left = vmem_call(
        lambda *refs: mix_kernel(chips, *refs),
        (
            turned,
            right,
            left,
            total,
            bias_mine,
            bias_theirs,
            og_mine,
            og_theirs,
            all_mixed,
        ),
        (
            shape(m, PLANE),
            shape(m, PLANE),
            shape(whole, PLANE),
            all_shape,
            shape(part, PLANE),
            shape(whole - part, PLANE),
        ),
        "mix",
        alias={8: 3},
    )

    weight_shape = shape(m, channels)
    weight_theirs, bias_part = vmem_call(
        weight_theirs_kernel,
        (pre_grad, all_mixed),
        (weight_shape, shape(GROUP, whole, jnp.float32)),
        "weight_theirs",
    )
    weight_far = swap(weight_theirs)
    bias_far = swap(bias_part[:, m:])
    act_far = swap(act_theirs)
    (weight_sum,) = vmem_call(
        weight_mine_kernel, (pre_grad, all_mixed, weight_far), (weight_shape,), "weight_mine"
    )
    together = patches == 2
    if together:
        weight_came = lax.ppermute(weight_sum, "patch", [(0, 1), (1, 0)])
    else:
        weight_grad = over_patches(weight_sum)
    (activated,) = vmem_call(
        join_kernel, (act_mine, act_far), (shape(m, DEPTH * PLANE),), "join"
    )
    for step in range(1, half_ring):
        right, left = [
            vmem_call(
                lambda *refs, step=step, half=half: pass_kernel(
                    chips, half_ring - step, half, *refs
                ),
                (turned, pre_grad, came),
                (shape(whole, PLANE),),
                "pass",
            )[0]
            for half, came in enumerate(send(right, left))
        ]
    right, left = send(right, left)
    mine, theirs = vmem_call(
        lambda *refs: last_kernel(chips, *refs),
        (turned, pre_grad, right, left, held(activated)),
        (shape(m, PLANE),) * 2,
        "last",
        free=(4,),
    )
    far = swap(theirs)

    (kernel_grad,) = vmem_call(
        tap_grad_kernel,
        (mine, far, vol_mine, wide_taps, bias_part, bias_far),
        (shape(TAPS + 1, m, jnp.float32),),
        "tap_grad",
        scratch=(
            pltpu.VMEM((DEPTH, m, PLANE), jnp.bfloat16),
            pltpu.VMEM((m, LANES), jnp.float32),
        ),
        free=(3,),
    )
    small_grad = over_patches(kernel_grad)
    kernel_grad, bias_grad = small_grad[:TAPS], small_grad[TAPS]
    weights, weight_outs, weight_scratch = (), (), ()
    if together:
        weights = (weight_sum, weight_came)
        weight_outs = (shape(m, channels, jnp.float32),)
        weight_scratch = (
            pltpu.VMEM((m, channels), jnp.float32),
            pltpu.SemaphoreType.DMA((m // STEP_ROWS,)),
        )
    volume_grad, *weight_made = vmem_call(
        lambda *refs: volume_grad_kernel(together, *refs),
        (mine, far, wide_taps, *weights),
        (shape(m, DEPTH * PLANE), *weight_outs),
        "volume_grad",
        scratch=weight_scratch,
        out_free=(1,),
    )
    if together:
        (weight_grad,) = weight_made
    return (
        activated[None],
        volume_grad[None],
        kernel_grad,
        weight_grad,
        bias_grad,
    )


def solution(mesh):
    placed = (
        P("patch", "chan", None),
        P(None, "chan"),
        P("chan", None),
        P("chan"),
        P("patch", "chan", None),
    )
    return jax.shard_map(
        body,
        mesh=mesh,
        in_specs=placed,
        out_specs=(
            P("patch", "chan", None),
            P("patch", "chan", None),
            P(None, "chan"),
            P("chan", None),
            P("chan"),
        ),
        check_vma=False,
    )
```

```python
import jax
import jax.numpy as jnp
from jax import lax
from jax.experimental import pallas as pl
from jax.experimental.pallas import tpu as pltpu
from jax.sharding import PartitionSpec as P

DEPTH = 2
ROWS = 16
SIDE = 32
PLANE = ROWS * SIDE
LANES = 128
VREGS = PLANE // LANES
GROUP = 8
STEP_ROWS = 16
TAPS = 27
TAP_ROWS = 32
BLOCK_ROWS = 64
MIB = 1024 * 1024


def chip_at(place, chips):
    return jnp.where(place < chips // 2, 2 * place, 2 * (chips - 1 - place) + 1)


def place_of(chip, chips):
    return jnp.where(chip % 2 == 0, chip // 2, chips - 1 - chip // 2)


def lane_index():
    return lax.broadcasted_iota(jnp.int32, (GROUP, LANES), 1)


def column_shift(tiles, step, lane):
    if step == 0:
        return tiles
    inside = lane % SIDE != (SIDE - 1 if step > 0 else 0)
    return [
        jnp.where(inside, pltpu.roll(tile, (-step) % LANES, 1), 0.0) for tile in tiles
    ]


def row_shift(tiles, step, lane):
    if step == 0:
        return tiles
    turned = [pltpu.roll(tile, (-step * SIDE) % LANES, 1) for tile in tiles]
    zero = jnp.zeros_like(tiles[0])
    if step > 0:
        ahead = turned[1:] + [zero]
        return [jnp.where(lane < LANES - SIDE, now, far) for now, far in zip(turned, ahead)]
    behind = [zero] + turned[:-1]
    return [jnp.where(lane >= SIDE, now, far) for now, far in zip(turned, behind)]


def tile_list(values):
    return [values[:, LANES * at : LANES * (at + 1)] for at in range(VREGS)]


def add_tiles(left, right):
    return right if left is None else [a + b for a, b in zip(left, right)]


def scale_tiles(column, tiles):
    wide = jnp.broadcast_to(column, (GROUP, LANES))
    return [wide * tile for tile in tiles]


def tap_columns(kernel_ref):
    taps = kernel_ref[...].astype(jnp.float32)
    core = lax.axis_index("chan") % 2
    down, same, up = taps[0:9], taps[9:18], taps[18:27]
    pad = jnp.zeros((TAP_ROWS - TAPS, taps.shape[1]), jnp.float32)
    order = [same, jnp.where(core == 0, up, down), jnp.where(core == 0, down, up), pad]
    return jnp.concatenate(order, axis=0).T


def spread_taps(kernel_ref, wide_ref):
    columns = tap_columns(kernel_ref)
    for t in range(wide_ref.shape[0]):
        wide_ref[t] = jnp.broadcast_to(columns[:, t : t + 1], (columns.shape[0], LANES))


def spread_kernel(kernel_ref, wide_ref):
    spread_taps(kernel_ref, wide_ref)


def depthwise_rows(vol_ref, wide_ref, at, core, lane):
    rows = pl.ds(at, STEP_ROWS)
    sources = [
        vol_ref[rows, pl.ds(pl.multiple_of(plane * PLANE, PLANE), PLANE)].astype(jnp.float32)
        for plane in (core, 1 - core)
    ]
    parts = []
    for low in range(0, STEP_ROWS, GROUP):
        group = pl.ds(at + low, GROUP)
        tiles = [tile_list(values[low : low + GROUP]) for values in sources]
        moved = [[column_shift(plane, c, lane) for c in (-1, 0, 1)] for plane in tiles]
        lines = [None] * 3
        for b in range(3):
            for side in range(2):
                for c in range(3):
                    wide = wide_ref[9 * side + 3 * b + c, group, :]
                    lines[b] = add_tiles(lines[b], [wide * tile for tile in moved[side][c]])
        shifted = [row_shift(lines[b], b - 1, lane) for b in (0, 2)]
        total = add_tiles(add_tiles(lines[1], shifted[0]), shifted[1])
        parts.append(jnp.concatenate(total, axis=1))
    return jnp.concatenate(parts, axis=0).astype(jnp.bfloat16)


def each_rows(m, step, unroll):
    size = min(unroll * STEP_ROWS, m)

    def run(index, carry):
        for at in range(0, size, STEP_ROWS):
            step(pl.multiple_of(index * size + at, STEP_ROWS))
        return carry

    lax.fori_loop(0, m // size, run, 0)


def depthwise_own_kernel(vol_hbm, kernel_hbm, out_ref, vol_ref, kernel_ref, wide_ref, sems):
    m = vol_ref.shape[0]
    rows = min(BLOCK_ROWS, m)
    core = lax.axis_index("chan") % 2
    lane = lane_index()
    taps_copy = pltpu.make_async_copy(kernel_hbm, kernel_ref, sems.at[0])
    taps_copy.start()
    copies = [
        pltpu.make_async_copy(
            vol_hbm.at[pl.ds(at, rows)], vol_ref.at[pl.ds(at, rows)], sems.at[1 + at // rows]
        )
        for at in range(0, m, rows)
    ]
    for copy in copies:
        copy.start()
    taps_copy.wait()
    spread_taps(kernel_ref, wide_ref)
    for block, copy in enumerate(copies):
        copy.wait()
        for at in range(block * rows, (block + 1) * rows, STEP_ROWS):
            out_ref[at : at + STEP_ROWS, :] = depthwise_rows(vol_ref, wide_ref, at, core, lane)


def depthwise_theirs_kernel(vol_ref, kernel_ref, own_ref, out_ref, wide_ref):
    m = vol_ref.shape[0]
    core = lax.axis_index("chan") % 2
    lane = lane_index()
    spread_taps(kernel_ref, wide_ref)
    out_ref[:m, :] = own_ref[...]

    def step(at):
        out_ref[pl.ds(m + at, STEP_ROWS), :] = depthwise_rows(vol_ref, wide_ref, at, core, lane)

    each_rows(m, step, 4)


VMEM_SPEC = pl.BlockSpec(memory_space=pltpu.VMEM)
HBM_SPEC = pl.BlockSpec(memory_space=pltpu.HBM)


ANY_SPEC = pl.BlockSpec(memory_space=pl.ANY)


def vmem_call(
    kernel, operands, outs, name, scratch=(), alias=None, free=(), hbm=False, out_free=()
):
    if hbm:
        operands = [pltpu.with_memory_space_constraint(x, pltpu.HBM) for x in operands]
    spec = HBM_SPEC if hbm else VMEM_SPEC
    return pl.pallas_call(
        kernel,
        out_shape=outs,
        in_specs=[ANY_SPEC if i in free else spec for i in range(len(operands))],
        out_specs=[HBM_SPEC if i in out_free else VMEM_SPEC for i in range(len(outs))],
        scratch_shapes=list(scratch),
        input_output_aliases=alias or {},
        compiler_params=pltpu.CompilerParams(vmem_limit_bytes=12 * MIB),
        name=name,
    )(*operands)


def held(values):
    return pltpu.with_memory_space_constraint(values, pltpu.HBM)


def position(chips):
    index = lax.axis_index("chan")
    return index % 2, index // 2, place_of(index // 2, chips)


def turn_kernel(mine, theirs, straight, turned):
    m = mine.shape[0]
    straight[:m, :] = mine[...]
    straight[m:, :] = theirs[...]
    turned[:, :m] = mine[...].T
    turned[:, m:] = theirs[...].T


def product(weights, block):
    return jnp.dot(weights, block, preferred_element_type=jnp.float32)


def stash(piece, low, all_ref, owner, core, m):
    high = low + piece.shape[0]
    for half in range(2):
        begin, end = max(low, half * m), min(high, (half + 1) * m)
        if begin >= end:
            continue
        side = core if half == 0 else 1 - core
        at = pl.multiple_of(owner * (2 * m) + side * m + (begin - half * m), STEP_ROWS)
        all_ref[pl.ds(at, end - begin), :] = piece[begin - low : end - low, :]


def assemble_kernel(chips, *refs):
    pieces = refs[: chips - 1]
    straight, total_ref, all_ref = refs[chips - 1 :]
    core, chip, place = position(chips)
    m = pieces[0].shape[0] // 2
    for number, piece in enumerate(pieces):
        distance = (number + 1) // 2
        back = chips - distance if number % 2 == 1 else distance
        owner = chip_at((place + back) % chips, chips)
        stash(piece, 0, all_ref, owner, core, m)
    opposite = chip_at((place + chips // 2) % chips, chips)
    blank = jnp.zeros((2 * m, all_ref.shape[1]), all_ref.dtype)
    all_ref[pl.ds(pl.multiple_of(opposite * (2 * m), 2 * m), 2 * m), :] = blank
    total_ref[...] = product(straight[...], all_ref[...])


def bias_column(ref):
    return jnp.broadcast_to(ref[...].astype(jnp.float32), (GROUP, ref.shape[1])).T[:, 0:1]


def weight_rows(turned, owner, whole):
    return turned[pl.ds(pl.multiple_of(owner * whole, whole), whole), :]


def mix_kernel(
    chips,
    turned,
    right,
    left,
    total_ref,
    bias_mine,
    bias_theirs,
    og_mine,
    og_theirs,
    filled,
    act_mine,
    act_theirs,
    grad_ref,
    all_ref,
    right_ref,
    left_ref,
):
    core, _, place = position(chips)
    m = og_mine.shape[0]
    cut = right.shape[0]
    opposite = chip_at((place + chips // 2) % chips, chips)
    stash(right[...], 0, all_ref, opposite, core, m)
    stash(left[...], cut, all_ref, opposite, core, m)
    block = all_ref[pl.ds(pl.multiple_of(opposite * (2 * m), 2 * m), 2 * m), :]
    sums = total_ref[...] + lax.dot_general(
        weight_rows(turned, opposite, 2 * m),
        block,
        (((0,), (0,)), ((), ())),
        preferred_element_type=jnp.float32,
    )
    here = pl.ds(pl.multiple_of(core * PLANE, PLANE), PLANE)
    for half, (bias_ref, og_ref, act_ref) in enumerate(
        ((bias_mine, og_mine, act_mine), (bias_theirs, og_theirs, act_theirs))
    ):
        rows = slice(half * m, (half + 1) * m)
        pre = sums[rows] + bias_column(bias_ref)
        gate = jax.nn.sigmoid(pre)
        act_ref[...] = (pre * gate).astype(act_ref.dtype)
        grad = og_ref[:, here].astype(jnp.float32) * gate * (1.0 + pre * (1.0 - gate))
        grad_ref[rows, :] = grad.astype(grad_ref.dtype)
    share = product(weight_rows(turned, opposite, 2 * m), grad_ref[...])
    part = right_ref.shape[0]
    right_ref[...] = share[:part].astype(right_ref.dtype)
    left_ref[...] = share[part:].astype(left_ref.dtype)


def pass_kernel(chips, distance, half, turned, grad, came, out_ref):
    _, _, place = position(chips)
    whole = grad.shape[0]
    count = came.shape[0]
    ahead = distance if half == 0 else chips - distance
    owner = chip_at((place + ahead) % chips, chips)
    share = product(weight_rows(turned, owner, whole), grad[...])
    low = 0 if half == 0 else whole - count
    for begin, end in ((0, low), (low, low + count), (low + count, whole)):
        if begin < end:
            part = share[begin:end]
            if begin == low:
                part = part + came[...].astype(jnp.float32)
            out_ref[begin:end, :] = part.astype(out_ref.dtype)


def last_kernel(chips, turned, grad, right, left, made, mine_ref, theirs_ref):
    core, chip, _ = position(chips)
    m = mine_ref.shape[0]
    total = (
        product(weight_rows(turned, chip, 2 * m), grad[...])
        + right[...].astype(jnp.float32)
        + left[...].astype(jnp.float32)
    )
    mine_ref[...] = jnp.where(core == 0, total[:m], total[m:]).astype(mine_ref.dtype)
    theirs_ref[...] = jnp.where(core == 0, total[m:], total[:m]).astype(theirs_ref.dtype)


def join_kernel(mine, theirs, out_ref):
    core = lax.axis_index("chan") % 2
    for ref, plane in ((mine, core), (theirs, 1 - core)):
        out_ref[:, pl.ds(pl.multiple_of(plane * PLANE, PLANE), PLANE)] = ref[...]


LANE_PAIRS = (((1,), (1,)), ((), ()))


def weight_theirs_kernel(grad, all_ref, out_ref, bias_ref):
    m = out_ref.shape[0]
    out_ref[...] = lax.dot_general(
        grad[m:, :], all_ref[...], LANE_PAIRS, preferred_element_type=jnp.float32
    ).astype(out_ref.dtype)
    ones = jnp.ones((GROUP, PLANE), grad.dtype)
    bias_ref[...] = lax.dot_general(
        ones, grad[...], LANE_PAIRS, preferred_element_type=jnp.float32
    )


def weight_mine_kernel(grad, all_ref, came, out_ref):
    m = out_ref.shape[0]
    total = lax.dot_general(
        grad[:m, :], all_ref[...], LANE_PAIRS, preferred_element_type=jnp.float32
    )
    out_ref[...] = (total + came[...].astype(jnp.float32)).astype(out_ref.dtype)


def plane_order(core, chunks, planes):
    planes[core] = chunks[0][...]
    planes[1 - core] = chunks[1][...]


def tap_grad_kernel(
    near_ref, far_ref, vol_ref, spread, bias_ref, bias_far, out_ref, planes, sums
):
    m = vol_ref.shape[0]
    lane = lane_index()
    plane_order(lax.axis_index("chan") % 2, (near_ref, far_ref), planes)

    def group(at):
        rows = pl.ds(at, STEP_ROWS)
        vol = [
            vol_ref[rows, z * PLANE : (z + 1) * PLANE].astype(jnp.float32) for z in range(DEPTH)
        ]
        grad = [planes[z, rows, :].astype(jnp.float32) for z in range(DEPTH)]
        sum_parts = []
        for low in range(0, STEP_ROWS, GROUP):
            moved_vol = [
                [column_shift(tile_list(vol[z][low : low + GROUP]), c, lane) for c in (-1, 0, 1)]
                for z in range(DEPTH)
            ]
            moved_grad = [
                [row_shift(tile_list(grad[z][low : low + GROUP]), -b, lane) for b in (-1, 0, 1)]
                for z in range(DEPTH)
            ]
            collected = jnp.zeros((GROUP, LANES), jnp.float32)
            for a in (-1, 0, 1):
                for b in range(3):
                    for c in range(3):
                        t = 9 * (a + 1) + 3 * b + c
                        acc = None
                        for z in range(DEPTH):
                            if not 0 <= z + a < DEPTH:
                                continue
                            for left, right in zip(moved_grad[z][b], moved_vol[z + a][c]):
                                acc = left * right if acc is None else acc + left * right
                        collected = jnp.where(
                            lane == t, jnp.sum(acc, axis=1, keepdims=True), collected
                        )
            sum_parts.append(collected)
        sums[rows, :] = jnp.concatenate(sum_parts, axis=0)

    each_rows(m, group, 1)
    out_ref[:TAPS, :] = sums[...].T[:TAPS, :]
    out_ref[TAPS : TAPS + 1, :] = bias_ref[0:1, :m] + bias_far[0:1, :]

def volume_grad_kernel(together, near_ref, far_ref, wide_ref, *refs):
    if together:
        weight_mine, weight_came, out_ref, weight_out, weight_wide, sems = refs
    else:
        (out_ref,) = refs
    m = out_ref.shape[0]
    core = lax.axis_index("chan") % 2
    lane = lane_index()

    def weight_copy(number):
        rows = pl.ds(pl.multiple_of(number * STEP_ROWS, STEP_ROWS), STEP_ROWS)
        return pltpu.make_async_copy(weight_wide.at[rows], weight_out.at[rows], sems.at[number])

    def step(at):
        rows = pl.ds(at, STEP_ROWS)
        grads = [ref[rows, :].astype(jnp.float32) for ref in (near_ref, far_ref)]
        parts = [[], []]
        for low in range(0, STEP_ROWS, GROUP):
            group = pl.ds(at + low, GROUP)
            tiles = [tile_list(values[low : low + GROUP]) for values in grads]
            moved = [[row_shift(plane, 1 - b, lane) for b in range(3)] for plane in tiles]
            for p in range(2):
                columns = [None] * 3
                for c in range(3):
                    for b in range(3):
                        t = 3 * b + c
                        columns[c] = add_tiles(
                            columns[c], [wide_ref[t, group, :] * x for x in moved[p][b]]
                        )
                        u = 9 * (2 - p) + t
                        columns[c] = add_tiles(
                            columns[c], [wide_ref[u, group, :] * x for x in moved[1 - p][b]]
                        )
                shifted = [column_shift(columns[c], 1 - c, lane) for c in (0, 2)]
                total = add_tiles(add_tiles(columns[1], shifted[0]), shifted[1])
                parts[p].append(jnp.concatenate(total, axis=1))
        for p, plane in enumerate((core, 1 - core)):
            place = pl.multiple_of(plane * PLANE, PLANE)
            out_ref[rows, pl.ds(place, PLANE)] = jnp.concatenate(parts[p], axis=0).astype(
                out_ref.dtype
            )

        if together:
            weight_wide[rows, :] = weight_mine[rows, :].astype(jnp.float32) + weight_came[
                rows, :
            ].astype(jnp.float32)
            weight_copy(at // STEP_ROWS).start()

    each_rows(m, step, 2)
    if together:
        for number in range(m // STEP_ROWS):
            weight_copy(number).wait()


def body(volume, depth_kernel, mix_weight, mix_bias, out_grad):
    n = lax.axis_size("chan")
    patches = lax.axis_size("patch")
    chips = n // 2
    half_ring = chips // 2
    core = lax.axis_index("chan") % 2
    m, channels = mix_weight.shape
    whole = 2 * m

    ring = [2 * k if k < half_ring else 2 * (chips - 1 - k) + 1 for k in range(chips)]
    to_core = [(i, i ^ 1) for i in range(n)]
    to_right = [
        (2 * ring[k] + c, 2 * ring[(k + 1) % chips] + c) for k in range(chips) for c in range(2)
    ]
    to_left = [(target, source) for source, target in to_right]

    def shape(rows, columns, kind=jnp.bfloat16):
        return jax.ShapeDtypeStruct((rows, columns), kind)

    def swap(values):
        return lax.ppermute(values, "chan", to_core)

    def send(right, left):
        return lax.ppermute(right, "chan", to_right), lax.ppermute(left, "chan", to_left)

    def over_patches(values):
        if patches != 2:
            return lax.psum(values.astype(jnp.float32), "patch")
        came = lax.ppermute(values, "patch", [(0, 1), (1, 0)])
        return values.astype(jnp.float32) + came.astype(jnp.float32)

    block_rows = min(BLOCK_ROWS, m)
    vol_mine = volume[0]
    vol_theirs = swap(vol_mine)
    kernel_theirs = swap(depth_kernel)
    wide_scratch = pltpu.VMEM((2 * TAPS // 3, m, LANES), jnp.float32)
    (mixed_own,) = vmem_call(
        depthwise_own_kernel,
        (vol_mine, depth_kernel),
        (shape(m, PLANE),),
        "depthwise_own",
        scratch=(
            pltpu.VMEM(vol_mine.shape, jnp.bfloat16),
            pltpu.VMEM(depth_kernel.shape, jnp.bfloat16),
            wide_scratch,
            pltpu.SemaphoreType.DMA((1 + m // block_rows,)),
        ),
        hbm=True,
    )
    (mixed_in,) = vmem_call(
        depthwise_theirs_kernel,
        (vol_theirs, kernel_theirs, mixed_own),
        (shape(whole, PLANE),),
        "depthwise_theirs",
        scratch=(wide_scratch,),
    )

    bias_mine = mix_bias[None, :]
    bias_theirs = swap(bias_mine)
    og_mine = out_grad[0]
    og_theirs = swap(og_mine)
    straight, turned = vmem_call(
        turn_kernel,
        (mix_weight, swap(mix_weight)),
        (shape(whole, channels), shape(channels, whole)),
        "turn",
    )

    (wide_taps,) = vmem_call(
        spread_kernel,
        (depth_kernel,),
        (jax.ShapeDtypeStruct((TAPS, m, LANES), jnp.float32),),
        "spread",
    )

    all_shape = shape(channels, PLANE)
    cut = 5 * m // 4 // STEP_ROWS * STEP_ROWS
    part = m
    right = left = mixed_in
    pieces = [mixed_in]
    for step in range(1, half_ring):
        right, left = send(right, left)
        pieces += [right, left]
    right, left = send(right[:cut], left[cut:])
    total, all_mixed = vmem_call(
        lambda *refs: assemble_kernel(chips, *refs),
        (*pieces, straight),
        (shape(whole, PLANE, jnp.float32), all_shape),
        "assemble",
    )
    act_mine, act_theirs, pre_grad, all_mixed, right, left = vmem_call(
        lambda *refs: mix_kernel(chips, *refs),
        (
            turned,
            right,
            left,
            total,
            bias_mine,
            bias_theirs,
            og_mine,
            og_theirs,
            all_mixed,
        ),
        (
            shape(m, PLANE),
            shape(m, PLANE),
            shape(whole, PLANE),
            all_shape,
            shape(part, PLANE),
            shape(whole - part, PLANE),
        ),
        "mix",
        alias={8: 3},
    )

    weight_shape = shape(m, channels)
    weight_theirs, bias_part = vmem_call(
        weight_theirs_kernel,
        (pre_grad, all_mixed),
        (weight_shape, shape(GROUP, whole, jnp.float32)),
        "weight_theirs",
    )
    weight_far = swap(weight_theirs)
    bias_far = swap(bias_part[:, m:])
    act_far = swap(act_theirs)
    (weight_sum,) = vmem_call(
        weight_mine_kernel, (pre_grad, all_mixed, weight_far), (weight_shape,), "weight_mine"
    )
    together = patches == 2
    if together:
        weight_came = lax.ppermute(weight_sum, "patch", [(0, 1), (1, 0)])
    else:
        weight_grad = over_patches(weight_sum)
    (activated,) = vmem_call(
        join_kernel, (act_mine, act_far), (shape(m, DEPTH * PLANE),), "join"
    )
    for step in range(1, half_ring):
        right, left = [
            vmem_call(
                lambda *refs, step=step, half=half: pass_kernel(
                    chips, half_ring - step, half, *refs
                ),
                (turned, pre_grad, came),
                (shape(whole, PLANE),),
                "pass",
            )[0]
            for half, came in enumerate(send(right, left))
        ]
    right, left = send(right, left)
    mine, theirs = vmem_call(
        lambda *refs: last_kernel(chips, *refs),
        (turned, pre_grad, right, left, held(activated)),
        (shape(m, PLANE),) * 2,
        "last",
        free=(4,),
    )
    far = swap(theirs)

    (kernel_grad,) = vmem_call(
        tap_grad_kernel,
        (mine, far, vol_mine, wide_taps, bias_part, bias_far),
        (shape(TAPS + 1, m, jnp.float32),),
        "tap_grad",
        scratch=(
            pltpu.VMEM((DEPTH, m, PLANE), jnp.bfloat16),
            pltpu.VMEM((m, LANES), jnp.float32),
        ),
        free=(3,),
    )
    small_grad = over_patches(kernel_grad)
    kernel_grad, bias_grad = small_grad[:TAPS], small_grad[TAPS]
    weights, weight_outs, weight_scratch = (), (), ()
    if together:
        weights = (weight_sum, weight_came)
        weight_outs = (shape(m, channels, jnp.float32),)
        weight_scratch = (
            pltpu.VMEM((m, channels), jnp.float32),
            pltpu.SemaphoreType.DMA((m // STEP_ROWS,)),
        )
    volume_grad, *weight_made = vmem_call(
        lambda *refs: volume_grad_kernel(together, *refs),
        (mine, far, wide_taps, *weights),
        (shape(m, DEPTH * PLANE), *weight_outs),
        "volume_grad",
        scratch=weight_scratch,
        out_free=(1,),
    )
    if together:
        (weight_grad,) = weight_made
    return (
        activated[None],
        volume_grad[None],
        kernel_grad,
        weight_grad,
        bias_grad,
    )


def solution(mesh):
    placed = (
        P("patch", "chan", None),
        P(None, "chan"),
        P("chan", None),
        P("chan"),
        P("patch", "chan", None),
    )
    return jax.shard_map(
        body,
        mesh=mesh,
        in_specs=placed,
        out_specs=(
            P("patch", "chan", None),
            P("patch", "chan", None),
            P(None, "chan"),
            P("chan", None),
            P("chan"),
        ),
        check_vma=False,
    )
```

```python
import jax
import jax.numpy as jnp
from jax import lax
from jax.experimental import pallas as pl
from jax.experimental.pallas import tpu as pltpu
from jax.sharding import PartitionSpec as P

DEPTH = 2
ROWS = 16
SIDE = 32
PLANE = ROWS * SIDE
LANES = 128
VREGS = PLANE // LANES
GROUP = 8
STEP_ROWS = 16
TAPS = 27
TAP_ROWS = 32
BLOCK_ROWS = 64
MIB = 1024 * 1024


def chip_at(place, chips):
    return jnp.where(place < chips // 2, 2 * place, 2 * (chips - 1 - place) + 1)


def place_of(chip, chips):
    return jnp.where(chip % 2 == 0, chip // 2, chips - 1 - chip // 2)


def lane_index():
    return lax.broadcasted_iota(jnp.int32, (GROUP, LANES), 1)


def column_shift(tiles, step, lane):
    if step == 0:
        return tiles
    inside = lane % SIDE != (SIDE - 1 if step > 0 else 0)
    return [
        jnp.where(inside, pltpu.roll(tile, (-step) % LANES, 1), 0.0) for tile in tiles
    ]


def row_shift(tiles, step, lane):
    if step == 0:
        return tiles
    turned = [pltpu.roll(tile, (-step * SIDE) % LANES, 1) for tile in tiles]
    zero = jnp.zeros_like(tiles[0])
    if step > 0:
        ahead = turned[1:] + [zero]
        return [jnp.where(lane < LANES - SIDE, now, far) for now, far in zip(turned, ahead)]
    behind = [zero] + turned[:-1]
    return [jnp.where(lane >= SIDE, now, far) for now, far in zip(turned, behind)]


def tile_list(values):
    return [values[:, LANES * at : LANES * (at + 1)] for at in range(VREGS)]


def add_tiles(left, right):
    return right if left is None else [a + b for a, b in zip(left, right)]


def scale_tiles(column, tiles):
    wide = jnp.broadcast_to(column, (GROUP, LANES))
    return [wide * tile for tile in tiles]


def tap_columns(kernel_ref):
    taps = kernel_ref[...].astype(jnp.float32)
    core = lax.axis_index("chan") % 2
    down, same, up = taps[0:9], taps[9:18], taps[18:27]
    pad = jnp.zeros((TAP_ROWS - TAPS, taps.shape[1]), jnp.float32)
    order = [same, jnp.where(core == 0, up, down), jnp.where(core == 0, down, up), pad]
    return jnp.concatenate(order, axis=0).T


def spread_taps(kernel_ref, wide_ref):
    columns = tap_columns(kernel_ref)
    for t in range(wide_ref.shape[0]):
        wide_ref[t] = jnp.broadcast_to(columns[:, t : t + 1], (columns.shape[0], LANES))


def spread_kernel(kernel_ref, wide_ref):
    spread_taps(kernel_ref, wide_ref)


def depthwise_rows(vol_ref, wide_ref, at, core, lane):
    rows = pl.ds(at, STEP_ROWS)
    sources = [
        vol_ref[rows, pl.ds(pl.multiple_of(plane * PLANE, PLANE), PLANE)].astype(jnp.float32)
        for plane in (core, 1 - core)
    ]
    parts = []
    for low in range(0, STEP_ROWS, GROUP):
        group = pl.ds(at + low, GROUP)
        tiles = [tile_list(values[low : low + GROUP]) for values in sources]
        moved = [[column_shift(plane, c, lane) for c in (-1, 0, 1)] for plane in tiles]
        lines = [None] * 3
        for b in range(3):
            for side in range(2):
                for c in range(3):
                    wide = wide_ref[9 * side + 3 * b + c, group, :]
                    lines[b] = add_tiles(lines[b], [wide * tile for tile in moved[side][c]])
        shifted = [row_shift(lines[b], b - 1, lane) for b in (0, 2)]
        total = add_tiles(add_tiles(lines[1], shifted[0]), shifted[1])
        parts.append(jnp.concatenate(total, axis=1))
    return jnp.concatenate(parts, axis=0).astype(jnp.bfloat16)


def each_rows(m, step, unroll):
    size = min(unroll * STEP_ROWS, m)

    def run(index, carry):
        for at in range(0, size, STEP_ROWS):
            step(pl.multiple_of(index * size + at, STEP_ROWS))
        return carry

    lax.fori_loop(0, m // size, run, 0)


def depthwise_own_kernel(vol_hbm, kernel_hbm, out_ref, vol_ref, kernel_ref, wide_ref, sems):
    m = vol_ref.shape[0]
    rows = min(BLOCK_ROWS, m)
    core = lax.axis_index("chan") % 2
    lane = lane_index()
    taps_copy = pltpu.make_async_copy(kernel_hbm, kernel_ref, sems.at[0])
    taps_copy.start()
    copies = [
        pltpu.make_async_copy(
            vol_hbm.at[pl.ds(at, rows)], vol_ref.at[pl.ds(at, rows)], sems.at[1 + at // rows]
        )
        for at in range(0, m, rows)
    ]
    for copy in copies:
        copy.start()
    taps_copy.wait()
    spread_taps(kernel_ref, wide_ref)
    for block, copy in enumerate(copies):
        copy.wait()
        for at in range(block * rows, (block + 1) * rows, STEP_ROWS):
            out_ref[at : at + STEP_ROWS, :] = depthwise_rows(vol_ref, wide_ref, at, core, lane)


def depthwise_theirs_kernel(vol_ref, kernel_ref, own_ref, out_ref, wide_ref):
    m = vol_ref.shape[0]
    core = lax.axis_index("chan") % 2
    lane = lane_index()
    spread_taps(kernel_ref, wide_ref)
    out_ref[:m, :] = own_ref[...]

    def step(at):
        out_ref[pl.ds(m + at, STEP_ROWS), :] = depthwise_rows(vol_ref, wide_ref, at, core, lane)

    each_rows(m, step, 4)


VMEM_SPEC = pl.BlockSpec(memory_space=pltpu.VMEM)
HBM_SPEC = pl.BlockSpec(memory_space=pltpu.HBM)


ANY_SPEC = pl.BlockSpec(memory_space=pl.ANY)


def vmem_call(
    kernel, operands, outs, name, scratch=(), alias=None, free=(), hbm=False, out_free=()
):
    if hbm:
        operands = [pltpu.with_memory_space_constraint(x, pltpu.HBM) for x in operands]
    spec = HBM_SPEC if hbm else VMEM_SPEC
    return pl.pallas_call(
        kernel,
        out_shape=outs,
        in_specs=[ANY_SPEC if i in free else spec for i in range(len(operands))],
        out_specs=[HBM_SPEC if i in out_free else VMEM_SPEC for i in range(len(outs))],
        scratch_shapes=list(scratch),
        input_output_aliases=alias or {},
        compiler_params=pltpu.CompilerParams(vmem_limit_bytes=12 * MIB),
        name=name,
    )(*operands)


def held(values):
    return pltpu.with_memory_space_constraint(values, pltpu.HBM)


def position(chips):
    index = lax.axis_index("chan")
    return index % 2, index // 2, place_of(index // 2, chips)


def turn_kernel(mine, theirs, straight, turned):
    m = mine.shape[0]
    straight[:m, :] = mine[...]
    straight[m:, :] = theirs[...]
    turned[:, :m] = mine[...].T
    turned[:, m:] = theirs[...].T


def product(weights, block):
    return jnp.dot(weights, block, preferred_element_type=jnp.float32)


def stash(piece, low, all_ref, owner, core, m):
    high = low + piece.shape[0]
    for half in range(2):
        begin, end = max(low, half * m), min(high, (half + 1) * m)
        if begin >= end:
            continue
        side = core if half == 0 else 1 - core
        at = pl.multiple_of(owner * (2 * m) + side * m + (begin - half * m), STEP_ROWS)
        all_ref[pl.ds(at, end - begin), :] = piece[begin - low : end - low, :]


def assemble_kernel(chips, *refs):
    pieces = refs[: chips - 1]
    straight, total_ref, all_ref = refs[chips - 1 :]
    core, chip, place = position(chips)
    m = pieces[0].shape[0] // 2
    for number, piece in enumerate(pieces):
        distance = (number + 1) // 2
        back = chips - distance if number % 2 == 1 else distance
        owner = chip_at((place + back) % chips, chips)
        stash(piece, 0, all_ref, owner, core, m)
    opposite = chip_at((place + chips // 2) % chips, chips)
    blank = jnp.zeros((2 * m, all_ref.shape[1]), all_ref.dtype)
    all_ref[pl.ds(pl.multiple_of(opposite * (2 * m), 2 * m), 2 * m), :] = blank
    total_ref[...] = product(straight[...], all_ref[...])


def bias_column(ref):
    return jnp.broadcast_to(ref[...].astype(jnp.float32), (GROUP, ref.shape[1])).T[:, 0:1]


def weight_rows(turned, owner, whole):
    return turned[pl.ds(pl.multiple_of(owner * whole, whole), whole), :]


def mix_kernel(
    chips,
    turned,
    right,
    left,
    total_ref,
    bias_mine,
    bias_theirs,
    og_mine,
    og_theirs,
    filled,
    act_mine,
    act_theirs,
    grad_ref,
    all_ref,
    right_ref,
    left_ref,
):
    core, _, place = position(chips)
    m = og_mine.shape[0]
    cut = right.shape[0]
    opposite = chip_at((place + chips // 2) % chips, chips)
    stash(right[...], 0, all_ref, opposite, core, m)
    stash(left[...], cut, all_ref, opposite, core, m)
    block = all_ref[pl.ds(pl.multiple_of(opposite * (2 * m), 2 * m), 2 * m), :]
    sums = total_ref[...] + lax.dot_general(
        weight_rows(turned, opposite, 2 * m),
        block,
        (((0,), (0,)), ((), ())),
        preferred_element_type=jnp.float32,
    )
    here = pl.ds(pl.multiple_of(core * PLANE, PLANE), PLANE)
    for half, (bias_ref, og_ref, act_ref) in enumerate(
        ((bias_mine, og_mine, act_mine), (bias_theirs, og_theirs, act_theirs))
    ):
        rows = slice(half * m, (half + 1) * m)
        pre = sums[rows] + bias_column(bias_ref)
        gate = jax.nn.sigmoid(pre)
        act_ref[...] = (pre * gate).astype(act_ref.dtype)
        grad = og_ref[:, here].astype(jnp.float32) * gate * (1.0 + pre * (1.0 - gate))
        grad_ref[rows, :] = grad.astype(grad_ref.dtype)
    share = product(weight_rows(turned, opposite, 2 * m), grad_ref[...])
    part = right_ref.shape[0]
    right_ref[...] = share[:part].astype(right_ref.dtype)
    left_ref[...] = share[part:].astype(left_ref.dtype)


def pass_kernel(chips, distance, half, turned, grad, came, out_ref):
    _, _, place = position(chips)
    whole = grad.shape[0]
    count = came.shape[0]
    ahead = distance if half == 0 else chips - distance
    owner = chip_at((place + ahead) % chips, chips)
    share = product(weight_rows(turned, owner, whole), grad[...])
    low = 0 if half == 0 else whole - count
    for begin, end in ((0, low), (low, low + count), (low + count, whole)):
        if begin < end:
            part = share[begin:end]
            if begin == low:
                part = part + came[...].astype(jnp.float32)
            out_ref[begin:end, :] = part.astype(out_ref.dtype)


def last_kernel(chips, turned, grad, right, left, made, mine_ref, theirs_ref):
    core, chip, _ = position(chips)
    m = mine_ref.shape[0]
    total = (
        product(weight_rows(turned, chip, 2 * m), grad[...])
        + right[...].astype(jnp.float32)
        + left[...].astype(jnp.float32)
    )
    mine_ref[...] = jnp.where(core == 0, total[:m], total[m:]).astype(mine_ref.dtype)
    theirs_ref[...] = jnp.where(core == 0, total[m:], total[:m]).astype(theirs_ref.dtype)


def join_kernel(mine, theirs, out_ref):
    core = lax.axis_index("chan") % 2
    for ref, plane in ((mine, core), (theirs, 1 - core)):
        out_ref[:, pl.ds(pl.multiple_of(plane * PLANE, PLANE), PLANE)] = ref[...]


LANE_PAIRS = (((1,), (1,)), ((), ()))


def weight_theirs_kernel(grad, all_ref, out_ref, bias_ref):
    m = out_ref.shape[0]
    out_ref[...] = lax.dot_general(
        grad[m:, :], all_ref[...], LANE_PAIRS, preferred_element_type=jnp.float32
    ).astype(out_ref.dtype)
    ones = jnp.ones((GROUP, PLANE), grad.dtype)
    bias_ref[...] = lax.dot_general(
        ones, grad[...], LANE_PAIRS, preferred_element_type=jnp.float32
    )


def weight_mine_kernel(grad, all_ref, came, out_ref):
    m = out_ref.shape[0]
    total = lax.dot_general(
        grad[:m, :], all_ref[...], LANE_PAIRS, preferred_element_type=jnp.float32
    )
    out_ref[...] = (total + came[...].astype(jnp.float32)).astype(out_ref.dtype)


def plane_order(core, chunks, planes):
    planes[core] = chunks[0][...]
    planes[1 - core] = chunks[1][...]


def tap_grad_kernel(
    near_ref, far_ref, vol_ref, spread, bias_ref, bias_far, out_ref, planes, sums
):
    m = vol_ref.shape[0]
    lane = lane_index()
    plane_order(lax.axis_index("chan") % 2, (near_ref, far_ref), planes)

    def group(at):
        rows = pl.ds(at, STEP_ROWS)
        vol = [
            vol_ref[rows, z * PLANE : (z + 1) * PLANE].astype(jnp.float32) for z in range(DEPTH)
        ]
        grad = [planes[z, rows, :].astype(jnp.float32) for z in range(DEPTH)]
        sum_parts = []
        for low in range(0, STEP_ROWS, GROUP):
            moved_vol = [
                [column_shift(tile_list(vol[z][low : low + GROUP]), c, lane) for c in (-1, 0, 1)]
                for z in range(DEPTH)
            ]
            moved_grad = [
                [row_shift(tile_list(grad[z][low : low + GROUP]), -b, lane) for b in (-1, 0, 1)]
                for z in range(DEPTH)
            ]
            collected = jnp.zeros((GROUP, LANES), jnp.float32)
            for a in (-1, 0, 1):
                for b in range(3):
                    for c in range(3):
                        t = 9 * (a + 1) + 3 * b + c
                        acc = None
                        for z in range(DEPTH):
                            if not 0 <= z + a < DEPTH:
                                continue
                            for left, right in zip(moved_grad[z][b], moved_vol[z + a][c]):
                                acc = left * right if acc is None else acc + left * right
                        collected = jnp.where(
                            lane == t, jnp.sum(acc, axis=1, keepdims=True), collected
                        )
            sum_parts.append(collected)
        sums[rows, :] = jnp.concatenate(sum_parts, axis=0)

    each_rows(m, group, 1)
    out_ref[:TAPS, :] = sums[...].T[:TAPS, :]
    out_ref[TAPS : TAPS + 1, :] = bias_ref[0:1, :m] + bias_far[0:1, :]

def volume_grad_kernel(together, near_ref, far_ref, wide_ref, *refs):
    if together:
        weight_mine, weight_came, out_ref, weight_out, weight_wide, sems = refs
    else:
        (out_ref,) = refs
    m = out_ref.shape[0]
    core = lax.axis_index("chan") % 2
    lane = lane_index()

    def weight_copy(number):
        rows = pl.ds(pl.multiple_of(number * STEP_ROWS, STEP_ROWS), STEP_ROWS)
        return pltpu.make_async_copy(weight_wide.at[rows], weight_out.at[rows], sems.at[number])

    def step(at):
        rows = pl.ds(at, STEP_ROWS)
        grads = [ref[rows, :].astype(jnp.float32) for ref in (near_ref, far_ref)]
        parts = [[], []]
        for low in range(0, STEP_ROWS, GROUP):
            group = pl.ds(at + low, GROUP)
            tiles = [tile_list(values[low : low + GROUP]) for values in grads]
            moved = [[row_shift(plane, 1 - b, lane) for b in range(3)] for plane in tiles]
            for p in range(2):
                columns = [None] * 3
                for c in range(3):
                    for b in range(3):
                        t = 3 * b + c
                        columns[c] = add_tiles(
                            columns[c], [wide_ref[t, group, :] * x for x in moved[p][b]]
                        )
                        u = 9 * (2 - p) + t
                        columns[c] = add_tiles(
                            columns[c], [wide_ref[u, group, :] * x for x in moved[1 - p][b]]
                        )
                shifted = [column_shift(columns[c], 1 - c, lane) for c in (0, 2)]
                total = add_tiles(add_tiles(columns[1], shifted[0]), shifted[1])
                parts[p].append(jnp.concatenate(total, axis=1))
        for p, plane in enumerate((core, 1 - core)):
            place = pl.multiple_of(plane * PLANE, PLANE)
            out_ref[rows, pl.ds(place, PLANE)] = jnp.concatenate(parts[p], axis=0).astype(
                out_ref.dtype
            )

        if together:
            weight_wide[rows, :] = weight_mine[rows, :].astype(jnp.float32) + weight_came[
                rows, :
            ].astype(jnp.float32)
            weight_copy(at // STEP_ROWS).start()

    each_rows(m, step, 2)
    if together:
        for number in range(m // STEP_ROWS):
            weight_copy(number).wait()


def body(volume, depth_kernel, mix_weight, mix_bias, out_grad):
    n = lax.axis_size("chan")
    patches = lax.axis_size("patch")
    chips = n // 2
    half_ring = chips // 2
    core = lax.axis_index("chan") % 2
    m, channels = mix_weight.shape
    whole = 2 * m

    ring = [2 * k if k < half_ring else 2 * (chips - 1 - k) + 1 for k in range(chips)]
    to_core = [(i, i ^ 1) for i in range(n)]
    to_right = [
        (2 * ring[k] + c, 2 * ring[(k + 1) % chips] + c) for k in range(chips) for c in range(2)
    ]
    to_left = [(target, source) for source, target in to_right]

    def shape(rows, columns, kind=jnp.bfloat16):
        return jax.ShapeDtypeStruct((rows, columns), kind)

    def swap(values):
        return lax.ppermute(values, "chan", to_core)

    def send(right, left):
        return lax.ppermute(right, "chan", to_right), lax.ppermute(left, "chan", to_left)

    def over_patches(values):
        if patches != 2:
            return lax.psum(values.astype(jnp.float32), "patch")
        came = lax.ppermute(values, "patch", [(0, 1), (1, 0)])
        return values.astype(jnp.float32) + came.astype(jnp.float32)

    block_rows = min(BLOCK_ROWS, m)
    vol_mine = volume[0]
    vol_theirs = swap(vol_mine)
    kernel_theirs = swap(depth_kernel)
    wide_scratch = pltpu.VMEM((2 * TAPS // 3, m, LANES), jnp.float32)
    (mixed_own,) = vmem_call(
        depthwise_own_kernel,
        (vol_mine, depth_kernel),
        (shape(m, PLANE),),
        "depthwise_own",
        scratch=(
            pltpu.VMEM(vol_mine.shape, jnp.bfloat16),
            pltpu.VMEM(depth_kernel.shape, jnp.bfloat16),
            wide_scratch,
            pltpu.SemaphoreType.DMA((1 + m // block_rows,)),
        ),
        hbm=True,
    )
    (mixed_in,) = vmem_call(
        depthwise_theirs_kernel,
        (vol_theirs, kernel_theirs, mixed_own),
        (shape(whole, PLANE),),
        "depthwise_theirs",
        scratch=(wide_scratch,),
    )

    bias_mine = mix_bias[None, :]
    bias_theirs = swap(bias_mine)
    og_mine = out_grad[0]
    og_theirs = swap(og_mine)
    straight, turned = vmem_call(
        turn_kernel,
        (mix_weight, swap(mix_weight)),
        (shape(whole, channels), shape(channels, whole)),
        "turn",
    )

    (wide_taps,) = vmem_call(
        spread_kernel,
        (depth_kernel,),
        (jax.ShapeDtypeStruct((TAPS, m, LANES), jnp.float32),),
        "spread",
    )

    all_shape = shape(channels, PLANE)
    cut = 11 * m // 8 // STEP_ROWS * STEP_ROWS
    part = m
    right = left = mixed_in
    pieces = [mixed_in]
    for step in range(1, half_ring):
        right, left = send(right, left)
        pieces += [right, left]
    right, left = send(right[:cut], left[cut:])
    total, all_mixed = vmem_call(
        lambda *refs: assemble_kernel(chips, *refs),
        (*pieces, straight),
        (shape(whole, PLANE, jnp.float32), all_shape),
        "assemble",
    )
    act_mine, act_theirs, pre_grad, all_mixed, right, left = vmem_call(
        lambda *refs: mix_kernel(chips, *refs),
        (
            turned,
            right,
            left,
            total,
            bias_mine,
            bias_theirs,
            og_mine,
            og_theirs,
            all_mixed,
        ),
        (
            shape(m, PLANE),
            shape(m, PLANE),
            shape(whole, PLANE),
            all_shape,
            shape(part, PLANE),
            shape(whole - part, PLANE),
        ),
        "mix",
        alias={8: 3},
    )

    weight_shape = shape(m, channels)
    weight_theirs, bias_part = vmem_call(
        weight_theirs_kernel,
        (pre_grad, all_mixed),
        (weight_shape, shape(GROUP, whole, jnp.float32)),
        "weight_theirs",
    )
    weight_far = swap(weight_theirs)
    bias_far = swap(bias_part[:, m:])
    act_far = swap(act_theirs)
    (weight_sum,) = vmem_call(
        weight_mine_kernel, (pre_grad, all_mixed, weight_far), (weight_shape,), "weight_mine"
    )
    together = patches == 2
    if together:
        weight_came = lax.ppermute(weight_sum, "patch", [(0, 1), (1, 0)])
    else:
        weight_grad = over_patches(weight_sum)
    (activated,) = vmem_call(
        join_kernel, (act_mine, act_far), (shape(m, DEPTH * PLANE),), "join"
    )
    for step in range(1, half_ring):
        right, left = [
            vmem_call(
                lambda *refs, step=step, half=half: pass_kernel(
                    chips, half_ring - step, half, *refs
                ),
                (turned, pre_grad, came),
                (shape(whole, PLANE),),
                "pass",
            )[0]
            for half, came in enumerate(send(right, left))
        ]
    right, left = send(right, left)
    mine, theirs = vmem_call(
        lambda *refs: last_kernel(chips, *refs),
        (turned, pre_grad, right, left, held(activated)),
        (shape(m, PLANE),) * 2,
        "last",
        free=(4,),
    )
    far = swap(theirs)

    (kernel_grad,) = vmem_call(
        tap_grad_kernel,
        (mine, far, vol_mine, wide_taps, bias_part, bias_far),
        (shape(TAPS + 1, m, jnp.float32),),
        "tap_grad",
        scratch=(
            pltpu.VMEM((DEPTH, m, PLANE), jnp.bfloat16),
            pltpu.VMEM((m, LANES), jnp.float32),
        ),
        free=(3,),
    )
    small_grad = over_patches(kernel_grad)
    kernel_grad, bias_grad = small_grad[:TAPS], small_grad[TAPS]
    weights, weight_outs, weight_scratch = (), (), ()
    if together:
        weights = (weight_sum, weight_came)
        weight_outs = (shape(m, channels, jnp.float32),)
        weight_scratch = (
            pltpu.VMEM((m, channels), jnp.float32),
            pltpu.SemaphoreType.DMA((m // STEP_ROWS,)),
        )
    volume_grad, *weight_made = vmem_call(
        lambda *refs: volume_grad_kernel(together, *refs),
        (mine, far, wide_taps, *weights),
        (shape(m, DEPTH * PLANE), *weight_outs),
        "volume_grad",
        scratch=weight_scratch,
        out_free=(1,),
    )
    if together:
        (weight_grad,) = weight_made
    return (
        activated[None],
        volume_grad[None],
        kernel_grad,
        weight_grad,
        bias_grad,
    )


def solution(mesh):
    placed = (
        P("patch", "chan", None),
        P(None, "chan"),
        P("chan", None),
        P("chan"),
        P("patch", "chan", None),
    )
    return jax.shard_map(
        body,
        mesh=mesh,
        in_specs=placed,
        out_specs=(
            P("patch", "chan", None),
            P("patch", "chan", None),
            P(None, "chan"),
            P("chan", None),
            P("chan"),
        ),
        check_vma=False,
    )
```
